256 devices in a mesh: seq: 64 (over z_lo, x, y, core), tp: 4 (over z_hi).
Axes of the slice: x: 4, y: 4, z: 8 (z_hi: 4, z_lo: 2; z = z_hi * 2 + z_lo), core: 2. Of those that a mesh axis runs over, the one named last changes fastest.
Arguments:
- code_ids: int32 [4, 8192], P(None, 'seq'), may hold values from 0 to 1023
- delays: int32 [4], replicated, may hold values from 0 to 3, as said below
- embed_table: bfloat16 [4, 1024, 2048], P(None, None, 'tp'), may hold values from -2.5 to 2.5
- project_in: bfloat16 [2048, 3, 2048], P(None, None, 'tp'), may hold values from -8 to 8
- project_out: bfloat16 [2048, 2048], P('tp'), may hold values from -0.125 to 0.125
- grad_output: bfloat16 [8192, 2048], P('seq', 'tp'), may hold values from -6 to 6
Outputs:
- layer_output: bfloat16 [8192, 2048], P('seq', 'tp')
- grad_embed: float32 [8192, 2048], P('seq', 'tp')
- grad_project_out: float32 [2048, 2048], P('tp', 'seq')
The draws below stay inside these ranges and needn't reach their ends.
Inputs may be any that keep to these rules, and one draw needn't show every extreme that they name: `delays`: at least one codebook has exactly 3.
All inputs are finite; a program needn't handle non-finite values.
Results may differ from the reference program's by a relative error of at most 0.035.
Values may be sent and summed in bfloat16 or wider, within the bound.
No kernel may reach another device: no remote copies, remote signals or barrier semaphores. Data moves between devices by JAX's collectives and lax.ppermute only.
A program may use at most 128 MiB of HBM per device.

```python
import jax
import jax.numpy as jnp
from jax import lax

D = 2048
HEADS = 32
HD = 64
V = 1024
BOOKS = 4
DMAX = 3
TOKENS = 8192


def draw_delays(key, part):
    key = jax.random.fold_in(key, 5)
    drawn = jax.random.randint(jax.random.fold_in(key, 1), (BOOKS,), 0, DMAX + 1)
    chosen = jax.random.randint(jax.random.fold_in(key, 2), (), 0, BOOKS)
    return jnp.where(jnp.arange(BOOKS) == chosen, DMAX, drawn).astype(jnp.int32)


def draw_project_in(key, part):
    key = jax.random.fold_in(key, 11)
    spread = D ** (-0.5)
    drawn = jax.random.normal(key, (D, 3, HEADS * HD), jnp.float32) * spread
    drawn = jnp.clip(drawn, -6.0 * spread, 6.0 * spread)
    return drawn.astype(jnp.bfloat16)


def plant(values, key, low, high):
    place = [jax.random.randint(jax.random.fold_in(key, axis), (), 0, length) for axis, length in enumerate(values.shape)]
    main_axis = values.shape.index(max(values.shape))
    beside = place[:main_axis] + [(place[main_axis] + 1) % values.shape[main_axis]] + place[main_axis + 1:]
    return values.at[tuple(place)].set(low).at[tuple(beside)].set(high)


def steps_of(key, dims, pieces, smallest, largest):
    factor_of = 1.0
    for dim, shards_of in pieces:
        draws = jax.random.uniform(jax.random.fold_in(jax.random.fold_in(key, 6), dim), (shards_of,), jnp.float32, smallest / len(pieces), largest / len(pieces))
        factor_of = factor_of * jnp.repeat(jnp.exp(draws), dims[dim] // shards_of).reshape((-1,) + (1,) * (len(dims) - 1 - dim))
    return factor_of


def noise(rng, shape, scale, limit, pieces=(), kind=jnp.bfloat16):
    entries = scale * jax.random.normal(rng, shape, jnp.float32)
    if pieces:
        entries = entries * steps_of(rng, shape, pieces, -0.22, 0.18)
    return jnp.clip(entries, -limit, limit).astype(kind)


def setup_inputs(seed: int = 0) -> dict:
    key_of = jax.random.split(jax.random.key(seed), 7)
    return {
        "code_ids": plant(jax.random.randint(key_of[0], (BOOKS, TOKENS), 0, V), jax.random.fold_in(key_of[0], 1), 0, V - 1).astype(jnp.int32),
        "delays": draw_delays(jax.random.fold_in(key_of[6], 71), 0),
        "embed_table": noise(key_of[2], (BOOKS, V, D), 0.3, 2.5, ((2, 4),)),
        "project_in": draw_project_in(jax.random.fold_in(key_of[6], 71), 0),
        "project_out": noise(key_of[4], (HEADS * HD, D), (HEADS * HD) ** -0.5, 0.125, ((0, 4),)),
        "grad_output": noise(key_of[5], (TOKENS, D), 1.0, 6.0, ((0, 64), (1, 4))),
    }


NEGATIVE = -1e+30

def contract(left_side, right_side, left_axis, right_axis):
    return lax.dot_general(left_side, right_side, (((left_axis,), (right_axis,)), ((), ())), preferred_element_type=jnp.float32)

def reference(code_ids, delays, embed_table, project_in, project_out, grad_output):
    positions = jnp.arange(TOKENS, dtype=jnp.int32)
    scaling = HD ** (-0.5)
    embedded = jnp.zeros((TOKENS, D), jnp.float32)
    for codebook in range(BOOKS):
        source = positions - delays[codebook]
        picked = code_ids[codebook][jnp.maximum(source, 0)]
        looked = embed_table[codebook][picked].astype(jnp.float32)
        embedded = embedded + jnp.where((source >= 0)[:, None], looked, 0.0)
    summed = embedded.astype(jnp.bfloat16)
    features = summed.astype(jnp.float32)
    inv_rms = lax.rsqrt(lax.optimization_barrier(jnp.mean(features * features, axis=1)) + 1e-05)
    normed = features * inv_rms[:, None]
    flat_in = project_in.reshape(D, 3 * HEADS * HD)
    projected = jnp.dot(normed.astype(jnp.bfloat16), flat_in, preferred_element_type=jnp.float32).astype(jnp.bfloat16)
    split_heads = projected.reshape(TOKENS, 3, HEADS, HD).transpose(1, 2, 0, 3)
    allowed = positions[None, :] <= positions[:, None]

    def head_forward(inputs):
        queries, key_rows, value_rows = inputs
        scores = jnp.where(allowed, contract(queries, key_rows, 1, 1) * scaling, NEGATIVE)
        row_top = lax.optimization_barrier(jnp.max(scores, axis=1))
        weights = jnp.where(allowed, jnp.exp(scores - row_top[:, None]), 0.0)
        row_total = lax.optimization_barrier(jnp.sum(weights, axis=1))
        mixed_rows = jnp.dot(weights.astype(jnp.bfloat16), value_rows, preferred_element_type=jnp.float32)
        return ((mixed_rows / row_total[:, None]).astype(jnp.bfloat16), row_top + jnp.log(row_total))
    attended, log_total = lax.map(head_forward, (split_heads[0], split_heads[1], split_heads[2]))
    attention = attended.transpose(1, 0, 2).reshape(TOKENS, HEADS * HD)
    projection = jnp.dot(attention, project_out, preferred_element_type=jnp.float32)
    layer_output = (features + projection).astype(jnp.bfloat16)
    grad_project_out = contract(attention, grad_output, 0, 0)
    grad_attention = contract(grad_output, project_out, 1, 1).astype(jnp.bfloat16)
    grad_heads = grad_attention.reshape(TOKENS, HEADS, HD).transpose(1, 0, 2)
    deltas = lax.optimization_barrier(jnp.sum(grad_heads.astype(jnp.float32) * attended.astype(jnp.float32), axis=2))

    def head_backward(inputs):
        queries, key_rows, value_rows, grad_rows, log_row, delta_row = inputs
        scores = contract(queries, key_rows, 1, 1) * scaling
        chances = jnp.where(allowed, jnp.exp(scores - log_row[:, None]), 0.0)
        value_grad = contract(chances.astype(jnp.bfloat16), grad_rows, 0, 0)
        prob_grad = contract(grad_rows, value_rows, 1, 1)
        score_grad = (chances * (prob_grad - delta_row[:, None]) * scaling).astype(jnp.bfloat16)
        query_grad = jnp.dot(score_grad, key_rows, preferred_element_type=jnp.float32)
        key_grad = contract(score_grad, queries, 0, 0)
        return (query_grad.astype(jnp.bfloat16), key_grad.astype(jnp.bfloat16), value_grad.astype(jnp.bfloat16))
    triple = lax.map(head_backward, (split_heads[0], split_heads[1], split_heads[2], grad_heads, log_total, deltas))
    grad_triple = jnp.stack(triple, axis=0).transpose(2, 0, 1, 3).reshape(TOKENS, 3 * HEADS * HD)
    grad_normed = contract(grad_triple, flat_in, 1, 1)
    centre = lax.optimization_barrier(jnp.mean(grad_normed * normed, axis=1))
    grad_embed = grad_output.astype(jnp.float32) + inv_rms[:, None] * (grad_normed - normed * centre[:, None])
    return (layer_output, grad_embed, grad_project_out)
```

```python
import functools

import jax
import jax.numpy as jnp
from jax import lax
from jax.experimental import pallas as pl
from jax.experimental.pallas import tpu as pltpu
from jax.sharding import Mesh, PartitionSpec as P

SPLIT = (2, 4, 4, 2, 4)
AXES = ("zl", "x", "y", "core", "tp")
SEQ = ("zl", "x", "y", "core")
HEADS_OVER = ("zl", "x")

HD = 64
BOOKS = 4
DMAX = 3
VOCAB = 1024
ROWS = 128
WIDTH = 512
LOCAL = 8
TP = 4
MINE = LOCAL * ROWS
TILE = 256
NEGATIVE = -1e30
EPS = 1e-05
F32 = jnp.float32
BF16 = jnp.bfloat16
PARAMS = pltpu.CompilerParams(vmem_limit_bytes=56 * 1024 * 1024)


def mm(left, right, left_axis=1, right_axis=0):
    return lax.dot_general(
        left, right, (((left_axis,), (right_axis,)), ((), ())), preferred_element_type=F32
    )


def ring(distance, count):
    return [(i, (i + distance) % count) for i in range(count)]


def embed_kernel(ids_ref, table_ref, out_ref, total):
    book = pl.program_id(0)
    entries = lax.broadcasted_iota(jnp.int32, (ROWS, VOCAB), 1)
    chosen = jnp.where(entries == ids_ref[0], 1.0, 0.0).astype(BF16)
    looked = mm(chosen, table_ref[0])

    @pl.when(book == 0)
    def _():
        total[...] = looked

    @pl.when(book > 0)
    def _():
        total[...] += looked

    out_ref[...] = total[...].astype(BF16)


def embed(ids, table):
    return pl.pallas_call(
        embed_kernel,
        grid=(BOOKS,),
        in_specs=[
            pl.BlockSpec((1, ROWS, 1), lambda b: (b, 0, 0)),
            pl.BlockSpec((1, VOCAB, WIDTH), lambda b: (b, 0, 0)),
        ],
        out_specs=pl.BlockSpec((ROWS, WIDTH), lambda b: (0, 0)),
        out_shape=jax.ShapeDtypeStruct((ROWS, WIDTH), BF16),
        scratch_shapes=[pltpu.VMEM((ROWS, WIDTH), F32)],
        compiler_params=PARAMS,
        name="embed",
    )(ids, table)


def project_kernel(summed_ref, weight_ref, grad_ref, out_ref, inv_ref, normed, total):
    step = pl.program_id(0)

    @pl.when(step == 0)
    def _():
        squares = jnp.zeros((ROWS, 1), F32)
        for t in range(TP):
            part = summed_ref[t].astype(F32)
            squares += jnp.sum(part * part, axis=1, keepdims=True)
        inv = lax.rsqrt(squares / (TP * WIDTH) + EPS)
        inv_ref[...] = jnp.broadcast_to(inv, (ROWS, 128))
        for t in range(TP):
            normed[t] = (summed_ref[t].astype(F32) * inv).astype(BF16)
        total[...] = jnp.zeros_like(total)

    total[...] += mm(normed[step], weight_ref[...])

    @pl.when(step == TP - 1)
    def _():
        done = total[...].astype(BF16)
        grads = grad_ref[...]
        for h in range(LOCAL):
            q, k, v = (done[:, j * WIDTH + h * HD : j * WIDTH + (h + 1) * HD] for j in range(3))
            out_ref[h] = jnp.concatenate([k, v, q, grads[:, h * HD : (h + 1) * HD]], axis=1)


def project(summed_all, weight, grads):
    return pl.pallas_call(
        project_kernel,
        grid=(TP,),
        in_specs=[
            pl.BlockSpec((TP, ROWS, WIDTH), lambda s: (0, 0, 0)),
            pl.BlockSpec((WIDTH, 3 * WIDTH), lambda s: (s, 0)),
            pl.BlockSpec((ROWS, WIDTH), lambda s: (0, 0)),
        ],
        out_specs=[
            pl.BlockSpec((LOCAL, ROWS, 4 * HD), lambda s: (0, 0, 0)),
            pl.BlockSpec((ROWS, 128), lambda s: (0, 0)),
        ],
        out_shape=[
            jax.ShapeDtypeStruct((LOCAL, ROWS, 4 * HD), BF16),
            jax.ShapeDtypeStruct((ROWS, 128), F32),
        ],
        scratch_shapes=[
            pltpu.VMEM((TP, ROWS, WIDTH), BF16),
            pltpu.VMEM((ROWS, 3 * WIDTH), F32),
        ],
        compiler_params=PARAMS,
        name="project",
    )(summed_all, weight, grads)


def flip(block):
    return jnp.transpose(block.astype(F32))


def frame_gap():
    keys = lax.broadcasted_iota(jnp.int32, (TILE, TILE), 0)
    queries = lax.broadcasted_iota(jnp.int32, (TILE, TILE), 1)
    frame = lambda i: lax.shift_right_logical(i, 7) * (LOCAL * ROWS) + lax.bitwise_and(i, ROWS - 1)
    return frame(keys) - frame(queries)


def chunk_limit(place_ref, back, other):
    y, core = place_ref[0], place_ref[1]
    chunk = lax.bitwise_and(y - back, 3) * 2 + (1 - core if other else core)
    return (2 * y + core - chunk) * ROWS


def masked(scores, gap, limit):
    last = jnp.where(gap <= limit, scores[scores.shape[0] - TILE :], NEGATIVE)
    if scores.shape[0] == TILE:
        return last
    return jnp.concatenate([scores[: scores.shape[0] - TILE], last], axis=0)


def pack(rows):
    halves = rows.reshape(LOCAL, 2, HD, HD)
    return jnp.concatenate([halves[:, 0], halves[:, 1]], axis=2)


def forward_kernel(place_ref, mine_ref, same_ref, other_ref, out_ref, stat_ref, queries, total, top):
    mine = flip(mine_ref[:, 2 * HD :])
    feature = lax.broadcasted_iota(jnp.int32, (2 * HD, MINE), 0)
    queries[...] = jnp.where(feature < HD, mine * (HD**-0.5), 0.0).astype(BF16)
    total[...] = jnp.zeros_like(total)
    top[...] = jnp.full_like(top, NEGATIVE)
    gap = frame_gap()

    def visit(back, carried):
        for other, ref in enumerate((same_ref, other_ref)):
            limit = chunk_limit(place_ref, back, other)
            pair = ref[back]
            values = jnp.where(feature < HD, 1.0, flip(pair)).astype(BF16)
            for a in range(MINE // TILE):
                count, at = TILE * (a + 1), slice(TILE * a, TILE * (a + 1))
                scores = masked(mm(pair[:count], queries[:, at]), gap, limit)
                old = top[:, at]
                new = jnp.maximum(old, jnp.max(scores, axis=0, keepdims=True))
                weights = jnp.exp(scores - new).astype(BF16)
                total[:, at] = total[:, at] * jnp.exp(old - new) + mm(values[:, :count], weights)
                top[:, at] = new
        return carried

    lax.fori_loop(0, 4, visit, 0)
    row_total = total[0:1]
    attended = (total[HD:] / row_total).astype(BF16)
    stat_ref[0:1] = top[...] + jnp.log(row_total)
    stat_ref[1:2] = jnp.sum(mine[HD:] * attended.astype(F32), axis=0, keepdims=True)
    out_ref[...] = pack(jnp.transpose(attended.astype(F32))).astype(BF16)


def full(*shape):
    return pl.BlockSpec(shape, lambda *_: (0,) * len(shape))


SMEM = pl.BlockSpec(memory_space=pltpu.SMEM)


def attend(place, mine, same, other):
    return pl.pallas_call(
        forward_kernel,
        in_specs=[
            SMEM,
            full(MINE, 4 * HD),
            full(4, MINE, 2 * HD),
            full(4, MINE, 2 * HD),
        ],
        out_specs=[full(LOCAL, HD, 2 * HD), full(8, MINE)],
        out_shape=[
            jax.ShapeDtypeStruct((LOCAL, HD, 2 * HD), BF16),
            jax.ShapeDtypeStruct((8, MINE), F32),
        ],
        scratch_shapes=[
            pltpu.VMEM((2 * HD, MINE), BF16),
            pltpu.VMEM((2 * HD, MINE), F32),
            pltpu.VMEM((1, MINE), F32),
        ],
        compiler_params=PARAMS,
        name="attend",
    )(place, mine, same, other)


def backward_kernel(
    place_ref, mine_ref, stat_ref, same_ref, other_ref,
    to_same_ref, to_other_ref, out_ref,
    columns, rows, query_total, pair_total,
):
    mine = mine_ref[:, 2 * HD :]
    first = lax.broadcasted_iota(jnp.int32, (MINE, 2 * HD), 1) < HD
    rows[0] = jnp.where(first, mine.astype(F32) * (HD**-0.5), 0.0).astype(BF16)
    rows[1] = jnp.where(first, 0.0, mine.astype(F32)).astype(BF16)
    columns[0] = flip(rows[0]).astype(BF16)
    columns[1] = flip(rows[1]).astype(BF16)
    query_total[...] = jnp.zeros_like(query_total)
    gap = frame_gap()

    def visit(back, carried):
        for other, (ref, to_ref) in enumerate(((same_ref, to_same_ref), (other_ref, to_other_ref))):
            limit = chunk_limit(place_ref, back, other)
            pair = ref[back]
            turned = flip(pair).astype(BF16)
            for a in reversed(range(MINE // TILE)):
                count, at = TILE * (a + 1), slice(TILE * a, TILE * (a + 1))
                scores = masked(mm(pair[:count], columns[0, :, at]), gap, limit)
                chances = jnp.exp(scores - stat_ref[0:1, at])
                grads = mm(pair[:count], columns[1, :, at])
                score_grad = (chances * (grads - stat_ref[1:2, at])).astype(BF16)
                query_total[:, at] += mm(turned[:, :count], score_grad)
                added = mm(score_grad, rows[0, at]) + mm(chances.astype(BF16), rows[1, at])
                if count == MINE:
                    pair_total[...] = added
                else:
                    pair_total[:count] += added
            to_ref[back] = pair_total[...].astype(BF16)
        return carried

    lax.fori_loop(0, 4, visit, 0)
    out_ref[...] = pack(jnp.transpose(query_total[:HD] * (HD**-0.5))).astype(BF16)


def attend_back(place, mine, stat, same, other):
    return pl.pallas_call(
        backward_kernel,
        in_specs=[
            SMEM,
            full(MINE, 4 * HD),
            full(8, MINE),
            full(4, MINE, 2 * HD),
            full(4, MINE, 2 * HD),
        ],
        out_specs=[full(4, MINE, 2 * HD), full(4, MINE, 2 * HD), full(LOCAL, HD, 2 * HD)],
        out_shape=[
            jax.ShapeDtypeStruct((4, MINE, 2 * HD), BF16),
            jax.ShapeDtypeStruct((4, MINE, 2 * HD), BF16),
            jax.ShapeDtypeStruct((LOCAL, HD, 2 * HD), BF16),
        ],
        scratch_shapes=[
            pltpu.VMEM((2, 2 * HD, MINE), BF16),
            pltpu.VMEM((2, MINE, 2 * HD), BF16),
            pltpu.VMEM((2 * HD, MINE), F32),
            pltpu.VMEM((MINE, 2 * HD), F32),
        ],
        compiler_params=PARAMS,
        name="attend_back",
    )(place, mine, stat, same, other)


def unpack(packed):
    return jnp.concatenate([packed[:, :HD], packed[:, HD:]], axis=0)


def output_kernel(heads_ref, grad_ref, weight_ref, share_ref, weight_grad_ref):
    attention = jnp.concatenate([unpack(heads_ref[h]) for h in range(LOCAL)], axis=1)
    for t in range(TP):
        at = slice(t * WIDTH, (t + 1) * WIDTH)
        share_ref[t] = mm(attention, weight_ref[:, at]).astype(BF16)
        weight_grad_ref[at] = mm(grad_ref[t], attention, 0, 0).astype(BF16)


def output_side(heads, grad_all, weight):
    return pl.pallas_call(
        output_kernel,
        in_specs=[full(LOCAL, HD, 2 * HD), full(TP, ROWS, WIDTH), full(WIDTH, TP * WIDTH)],
        out_specs=[full(TP, ROWS, WIDTH), full(TP * WIDTH, WIDTH)],
        out_shape=[
            jax.ShapeDtypeStruct((TP, ROWS, WIDTH), BF16),
            jax.ShapeDtypeStruct((TP * WIDTH, WIDTH), BF16),
        ],
        compiler_params=PARAMS,
        name="output_side",
    )(heads, grad_all, weight)


def weight_sum_kernel(parts_ref, out_ref):
    total = parts_ref[0].astype(F32)
    for i in range(1, parts_ref.shape[0]):
        total += parts_ref[i].astype(F32)
    out_ref[...] = jnp.transpose(total)


def weight_sum(parts):
    return pl.pallas_call(
        weight_sum_kernel,
        in_specs=[full(*parts.shape)],
        out_specs=full(WIDTH, parts.shape[1]),
        out_shape=jax.ShapeDtypeStruct((WIDTH, parts.shape[1]), F32),
        compiler_params=PARAMS,
        name="weight_sum",
    )(parts)


EXTRA = 16


def input_kernel(back_ref, weight_ref, summed_ref, inv_ref, out_ref, triple, centre):
    step = pl.program_id(0)

    @pl.when(step == 0)
    def _():
        pairs = [back_ref[h, :ROWS] for h in range(LOCAL)]
        parts = [unpack(back_ref[h, ROWS:]) for h in range(LOCAL)]
        parts += [pair[:, :HD] for pair in pairs] + [pair[:, HD:] for pair in pairs]
        triple[...] = jnp.concatenate(parts, axis=1)
        centre[...] = jnp.zeros_like(centre)

    part = mm(triple[...], weight_ref[...], 1, 1)
    normed = summed_ref[step].astype(F32) * inv_ref[:, 0:1]
    centre[...] += jnp.sum(part * normed, axis=1, keepdims=True)
    out_ref[step, :ROWS] = part.astype(BF16)

    @pl.when(step == TP - 1)
    def _():
        line = jnp.transpose(centre[...])[0:1]
        high = line.astype(BF16).astype(F32)
        middle = (line - high).astype(BF16).astype(F32)
        low = line - high - middle
        zero = jnp.zeros((1, ROWS), F32)
        block = jnp.concatenate([high, middle, low] + [zero] * (EXTRA - 3), axis=0)
        block = jnp.concatenate([block, jnp.zeros((EXTRA, WIDTH - ROWS), F32)], axis=1)
        for t in range(TP):
            out_ref[t, ROWS:] = block.astype(BF16)


def input_side(back, weight, summed_all, inv):
    return pl.pallas_call(
        input_kernel,
        grid=(TP,),
        in_specs=[
            full(LOCAL, ROWS + HD, 2 * HD),
            pl.BlockSpec((WIDTH, 3 * WIDTH), lambda s: (s, 0)),
            full(TP, ROWS, WIDTH),
            full(ROWS, 128),
        ],
        out_specs=full(TP, ROWS + EXTRA, WIDTH),
        out_shape=jax.ShapeDtypeStruct((TP, ROWS + EXTRA, WIDTH), BF16),
        scratch_shapes=[pltpu.VMEM((ROWS, 3 * WIDTH), BF16), pltpu.VMEM((ROWS, 128), F32)],
        compiler_params=PARAMS,
        name="input_side",
    )(back, weight, summed_all, inv)


def finish_kernel(parts_ref, summed_ref, inv_ref, grad_ref, out_ref):
    total = sum(parts_ref[t, :ROWS].astype(F32) for t in range(TP))
    lines = sum(parts_ref[t, ROWS:, :ROWS].astype(F32) for t in range(TP))
    line = jnp.sum(lines, axis=0, keepdims=True) / (TP * WIDTH)
    centre = jnp.transpose(jnp.broadcast_to(line, (ROWS, ROWS)))[:, 0:1]
    inv = inv_ref[:, 0:1]
    normed = summed_ref[...].astype(F32) * inv
    out_ref[...] = grad_ref[...].astype(F32) + inv * (total - normed * centre)


def finish(parts, summed, inv, grad):
    return pl.pallas_call(
        finish_kernel,
        in_specs=[
            full(TP, ROWS + EXTRA, WIDTH),
            full(ROWS, WIDTH),
            full(ROWS, 128),
            full(ROWS, WIDTH),
        ],
        out_specs=full(ROWS, WIDTH),
        out_shape=jax.ShapeDtypeStruct((ROWS, WIDTH), F32),
        compiler_params=PARAMS,
        name="finish",
    )(parts, summed, inv, grad)


def pick_ids(code_ids, delays):
    seq_index = lax.axis_index(SEQ)
    count = lax.axis_size(SEQ)
    route = [(i, i + 1) for i in range(count - 1)]
    before = lax.ppermute(code_ids[:, ROWS - DMAX :], SEQ, route)
    joined = jnp.concatenate([before, code_ids], axis=1)
    picked = joined[:, DMAX:]
    for delay in range(1, DMAX + 1):
        moved = joined[:, DMAX - delay : DMAX - delay + ROWS]
        picked = jnp.where(delays[:, None] == delay, moved, picked)
    frames = seq_index * ROWS + jnp.arange(ROWS, dtype=jnp.int32)
    return jnp.where(frames[None, :] >= delays[:, None], picked, -1)[:, :, None]


def body(code_ids, delays, embed_table, project_in, project_out, grad_output):
    place = jnp.stack([lax.axis_index("y"), lax.axis_index("core")]).astype(jnp.int32)
    weight_in = project_in.reshape(TP * WIDTH, 3 * WIDTH)
    grad_all = lax.all_gather(grad_output, "tp", axis=0)
    summed = embed(pick_ids(code_ids, delays), embed_table)
    summed_all = lax.all_gather(summed, "tp", axis=0)
    grad_attention = sum(
        mm(grad_all[t], project_out[:, t * WIDTH : (t + 1) * WIDTH], 1, 1) for t in range(TP)
    ).astype(BF16)
    blocks, inv = project(summed_all, weight_in, grad_attention)
    mine = lax.all_to_all(blocks, HEADS_OVER, 0, 0, tiled=True).reshape(MINE, 4 * HD)

    own = mine[:, : 2 * HD]
    same = jnp.stack([own] + [lax.ppermute(own, "y", ring(k, 4)) for k in range(1, 4)])
    other = lax.ppermute(same, "core", [(0, 1), (1, 0)])
    attended, stat = attend(place, mine, same, other)

    heads = lax.all_to_all(attended, HEADS_OVER, 0, 0, tiled=True)
    shares, weight_grads = output_side(heads, grad_all, project_out)
    shares = lax.all_to_all(shares, "tp", 0, 0, tiled=True)
    layer_output = (
        summed.astype(F32) + sum(shares[t].astype(F32) for t in range(TP))
    ).astype(BF16)
    weight_parts = lax.all_to_all(
        weight_grads.reshape(64, TP * WIDTH // 64, WIDTH), SEQ, 0, 0, tiled=True
    )
    grad_project_out = weight_sum(weight_parts)

    to_same, to_other, query_grads = attend_back(place, mine, stat, same, other)
    from_other = lax.ppermute(to_other, "core", [(0, 1), (1, 0)])
    both = (to_same.astype(F32) + from_other.astype(F32)).astype(BF16)
    pair_grads = both[0].astype(F32)
    for k in range(1, 4):
        pair_grads += lax.ppermute(both[k], "y", ring(-k, 4)).astype(F32)
    packed = jnp.concatenate(
        [pair_grads.astype(BF16).reshape(LOCAL, ROWS, 2 * HD), query_grads], axis=1
    )
    back = lax.all_to_all(packed, HEADS_OVER, 0, 0, tiled=True)
    parts = input_side(back, weight_in, summed_all, inv)
    parts = lax.all_to_all(parts, "tp", 0, 0, tiled=True)
    grad_embed = finish(parts, summed, inv, grad_output)
    return layer_output, grad_embed, grad_project_out


def solution(mesh):
    fine = Mesh(mesh.devices.reshape(SPLIT), AXES)
    return jax.shard_map(
        body,
        mesh=fine,
        in_specs=(
            P(None, SEQ),
            P(),
            P(None, None, "tp"),
            P(None, None, "tp"),
            P("tp", None),
            P(SEQ, "tp"),
        ),
        out_specs=(P(SEQ, "tp"), P(SEQ, "tp"), P("tp", SEQ)),
        check_vma=False,
    )
```

```python
import functools

import jax
import jax.numpy as jnp
from jax import lax
from jax.experimental import pallas as pl
from jax.experimental.pallas import tpu as pltpu
from jax.sharding import Mesh, PartitionSpec as P

SPLIT = (2, 4, 4, 2, 4)
AXES = ("zl", "x", "y", "core", "tp")
SEQ = ("zl", "x", "y", "core")
HEADS_OVER = ("zl", "x")

HD = 64
BOOKS = 4
DMAX = 3
VOCAB = 1024
ROWS = 128
WIDTH = 512
LOCAL = 8
TP = 4
COLUMNS = 32
BACK = ROWS + HD
MINE = LOCAL * ROWS
TILE = 256
NEGATIVE = -1e30
EPS = 1e-05
F32 = jnp.float32
BF16 = jnp.bfloat16
MIB = 1024 * 1024
COST = {"small": 4e9, "attend": 5e9}


def mm(left, right, left_axis=1, right_axis=0):
    return lax.dot_general(
        left, right, (((left_axis,), (right_axis,)), ((), ())), preferred_element_type=F32
    )


def ring(distance, count):
    return [(i, (i + distance) % count) for i in range(count)]


def vmem(count):
    return [pl.BlockSpec(memory_space=pltpu.VMEM)] * count


SMEM = pl.BlockSpec(memory_space=pltpu.SMEM)


def local(kernel, name, shapes, scratch=(), flops=0, place=True):
    def call(*args):
        outs = [jax.ShapeDtypeStruct(shape, kind) for shape, kind in shapes]
        moved = sum(a.size * a.dtype.itemsize for a in (*args, *outs))
        return pl.pallas_call(
            kernel,
            in_specs=([SMEM] if place else []) + vmem(len(args) - place),
            out_specs=vmem(len(outs)),
            out_shape=outs,
            scratch_shapes=list(scratch),
            compiler_params=pltpu.CompilerParams(vmem_limit_bytes=16 * MIB),
            cost_estimate=pl.CostEstimate(flops=int(flops), transcendentals=0, bytes_accessed=moved),
            name=name,
        )(*args)

    return call


def block_of(place_ref, step):
    return pl.ds(pl.multiple_of(lax.bitwise_and(place_ref[2] + step, 3) * WIDTH, WIDTH), WIDTH)


def fold(rows):
    return jnp.concatenate([rows[:HD], rows[HD:]], axis=1)


def unfold(folded):
    return jnp.concatenate([folded[:, :HD], folded[:, HD:]], axis=0)


def embed_kernel(ids_ref, table_ref, out_ref):
    entries = lax.broadcasted_iota(jnp.int32, (ROWS, VOCAB), 1)
    total = jnp.zeros((ROWS, WIDTH), F32)
    for book in range(BOOKS):
        chosen = jnp.where(entries == ids_ref[book], 1.0, 0.0).astype(BF16)
        total += mm(chosen, table_ref[book])
    out_ref[...] = total.astype(BF16)


def embed(ids, table):
    return local(embed_kernel, "embed", [((ROWS, WIDTH), BF16)], place=False)(ids, table)[0]


def grad_side_kernel(place_ref, g0, g1, g2, g3, weight_ref, out_ref):
    total = jnp.zeros((ROWS, WIDTH), F32)
    for back, ref in enumerate((g0, g1, g2, g3)):
        total += mm(ref[...], weight_ref[:, block_of(place_ref, -back)], 1, 1)
    for h in range(LOCAL):
        out_ref[h] = fold(total[:, h * HD : (h + 1) * HD]).astype(BF16)


def grad_side(place, grads, weight):
    call = local(grad_side_kernel, "grad_side", [((LOCAL, HD, 2 * HD), BF16)], flops=COST["small"])
    return call(place, *grads, weight)[0]


def project_kernel(place_ref, s0, s1, s2, s3, weight_ref, out_ref, done_ref, inv_ref):
    parts = [ref[...].astype(F32) for ref in (s0, s1, s2, s3)]
    squares = sum(jnp.sum(part * part, axis=1, keepdims=True) for part in parts)
    inv = lax.rsqrt(squares / (TP * WIDTH) + EPS)
    inv_ref[...] = jnp.broadcast_to(inv, (ROWS, 128))
    normed = [(part * inv).astype(BF16) for part in parts]
    done = []
    for j in range(3):
        total = jnp.zeros((ROWS, WIDTH), F32)
        for back in range(TP):
            total += mm(normed[back], weight_ref[j, block_of(place_ref, -back)])
        done.append(total.astype(BF16))
        done_ref[j] = done[j]
    for h in range(LOCAL):
        q, k, v = [part[:, h * HD : (h + 1) * HD] for part in done]
        out_ref[h, :ROWS] = jnp.concatenate([k, v], axis=1)
        out_ref[h, ROWS:] = fold(q)


def project(place, summeds, weight):
    shapes = [
        ((LOCAL, BACK, 2 * HD), BF16),
        ((3, ROWS, WIDTH), BF16),
        ((ROWS, 128), F32),
    ]
    call = local(project_kernel, "project", shapes, flops=COST["small"])
    return call(place, *summeds, weight)


def flip(block):
    return jnp.transpose(block.astype(F32))


def frame_gap():
    keys = lax.broadcasted_iota(jnp.int32, (TILE, TILE), 0)
    queries = lax.broadcasted_iota(jnp.int32, (TILE, TILE), 1)
    frame = lambda i: lax.shift_right_logical(i, 7) * (LOCAL * ROWS) + lax.bitwise_and(i, ROWS - 1)
    return frame(keys) - frame(queries)


def chunk_limit(place_ref, back, other):
    y, core = place_ref[0], place_ref[1]
    chunk = lax.bitwise_and(y - back, 3) * 2 + (1 - core if other else core)
    return (2 * y + core - chunk) * ROWS


STEPS = MINE // TILE


def part_of(a):
    return TILE * (a + 1), slice(TILE * a, TILE * (a + 1))


def masked(scores, gap, limit):
    last = jnp.where(gap <= limit, scores[scores.shape[0] - TILE :], NEGATIVE)
    if scores.shape[0] == TILE:
        return last
    return jnp.concatenate([scores[: scores.shape[0] - TILE], last], axis=0)


def pack(rows):
    halves = rows.reshape(LOCAL, 2, HD, HD)
    return jnp.concatenate([halves[:, 0], halves[:, 1]], axis=2)


def prepare_kernel(mine_ref, pair_ref, columns_ref):
    queries = [unfold(mine_ref[a, ROWS:]).astype(F32) for a in range(LOCAL)]
    queries = jnp.concatenate(queries, axis=0) * (HD**-0.5)
    wide = jnp.concatenate([queries, jnp.zeros((MINE, HD), F32)], axis=1)
    columns_ref[...] = jnp.transpose(wide).astype(BF16)
    for a in range(LOCAL):
        pair_ref[a * ROWS : (a + 1) * ROWS] = mine_ref[a, :ROWS]


def prepare(mine):
    shapes = [((MINE, 2 * HD), BF16), ((2 * HD, MINE), BF16)]
    return local(prepare_kernel, "prepare", shapes, place=False)(mine)


STATS = 48


def three_parts(row):
    block = jnp.concatenate([row[:, i * ROWS : (i + 1) * ROWS] for i in range(LOCAL)], axis=0)
    high = block.astype(BF16).astype(F32)
    middle = (block - high).astype(BF16).astype(F32)
    return jnp.concatenate([high, middle, block - high - middle], axis=0)


def whole_row(parts):
    block = parts[:LOCAL] + parts[LOCAL : 2 * LOCAL] + parts[2 * LOCAL :]
    return jnp.concatenate([block[i : i + 1] for i in range(LOCAL)], axis=1)


def prepare_back_kernel(mixed_ref, turned_ref, q_columns, stat_ref, both_ref, columns_ref, delta_ref):
    grads = [unfold(mixed_ref[a, HD:]).astype(F32) for a in range(LOCAL)]
    grads = jnp.concatenate(grads, axis=0)
    queries = jnp.transpose(q_columns[...].astype(F32))
    columns = jnp.transpose(jnp.concatenate([jnp.zeros((MINE, HD), F32), grads], axis=1))
    columns_ref[...] = columns.astype(BF16)
    both = columns[HD:] * turned_ref[...].astype(F32)
    delta = jnp.sum(both, axis=0, keepdims=True)
    delta_ref[...] = jnp.broadcast_to(delta, (8, MINE))
    both_ref[:MINE] = jnp.concatenate([queries[:, :HD], grads], axis=1).astype(BF16)
    stats = jnp.concatenate([three_parts(stat_ref[0:1]), three_parts(delta)], axis=0)
    both_ref[MINE:] = stats.astype(BF16)


def prepare_back(*args):
    shapes = [((MINE + STATS, 2 * HD), BF16), ((2 * HD, MINE), BF16), ((8, MINE), F32)]
    return local(prepare_back_kernel, "prepare_back", shapes, place=False)(*args)


def forward_kernel(which, first, last, place_ref, columns_ref, *refs):
    chunks, refs = refs[:2], refs[2:]
    if not first:
        (old_total, old_top), refs = refs[:2], refs[2:]
    if last:
        grad_ref, out_ref, turned_ref, stat_ref, total, top = refs
    else:
        total, top = refs
    if first:
        total[...] = jnp.zeros_like(total)
        top[...] = jnp.full_like(top, NEGATIVE)
    else:
        total[...] = old_total[...]
        top[...] = old_top[...]
    feature = lax.broadcasted_iota(jnp.int32, (2 * HD, MINE), 0)
    gap = frame_gap()
    limits = [chunk_limit(place_ref, back, other) for back, other in which]
    values = [jnp.where(feature < HD, 1.0, flip(ref[...])).astype(BF16) for ref in chunks]

    def scores_of(a):
        count, at = part_of(a)
        return [
            masked(mm(ref[:count], columns_ref[:, at]), gap, limit)
            for ref, limit in zip(chunks, limits, strict=True)
        ]

    scores = scores_of(0)
    for a in range(STEPS):
        now, scores = scores, scores_of(a + 1) if a + 1 < STEPS else None
        count, at = part_of(a)
        old = top[0:1, at]
        new = old
        for score in now:
            new = jnp.maximum(new, jnp.max(score, axis=0, keepdims=True))
        added = total[:, at] * jnp.exp(old - new)
        for score, value in zip(now, values, strict=True):
            added += mm(value[:, :count], jnp.exp(score - new).astype(BF16))
        total[:, at] = added
        top[0:1, at] = new
    if last:
        row_total = total[0:1]
        attended = (total[HD:] / row_total).astype(BF16).astype(F32)
        stat_ref[...] = jnp.broadcast_to(top[0:1] + jnp.log(row_total), (8, MINE))
        turned_ref[...] = attended.astype(BF16)
        out_ref[:, :HD] = pack(jnp.transpose(attended)).astype(BF16)
        out_ref[:, HD:] = grad_ref[...]


def attend(step, place, columns, group, state=(), grads=None):
    held = [((2 * HD, MINE), F32), ((8, MINE), F32)]
    last = grads is not None
    outs = [((LOCAL, ROWS, 2 * HD), BF16), ((HD, MINE), BF16), ((8, MINE), F32)]
    kernel = functools.partial(forward_kernel, [c[:2] for c in group], not state, last)
    return local(
        kernel,
        f"attend{step}",
        outs if last else held,
        scratch=[pltpu.VMEM(*h) for h in held] if last else [],
        flops=COST["attend"],
    )(place, columns, *[c[2] for c in group], *state, *([grads] if last else []))


def query_kernel(which, first, last, place_ref, q_columns, g_columns, stat_ref, delta_ref, *refs):
    chunks, refs = refs[: len(which)], refs[len(which) :]
    if not first:
        old_total, refs = refs[0], refs[1:]
    out_ref, total = refs[0], refs[-1]
    total[...] = jnp.zeros_like(total) if first else old_total[...]
    gap = frame_gap()
    limits = [chunk_limit(place_ref, back, other) for back, other in which]
    steps = [(i, a) for i in range(len(which)) for a in range(STEPS)]

    def products(i, a):
        count, at = part_of(a)
        pair = chunks[i][:count]
        return mm(pair, q_columns[:, at]), mm(pair, g_columns[:, at])

    ahead = products(*steps[0])
    for n, (i, a) in enumerate(steps):
        scores, grads = ahead
        if n + 1 < len(steps):
            ahead = products(*steps[n + 1])
        if a == 0:
            turned = flip(chunks[i][...]).astype(BF16)
        count, at = part_of(a)
        chances = jnp.exp(masked(scores, gap, limits[i]) - stat_ref[0:1, at])
        score_grad = (chances * (grads - delta_ref[0:1, at])).astype(BF16)
        total[:, at] += mm(turned[:, :count], score_grad)
    if last:
        out_ref[...] = pack(jnp.transpose(total[:HD] * (HD**-0.5))).astype(BF16)


def query_pass(step, place, held, group, state=None):
    last = state is not None
    kernel = functools.partial(query_kernel, [c[:2] for c in group], not last, last)
    return local(
        kernel,
        f"query_pass{step}",
        [((LOCAL, HD, 2 * HD), BF16) if last else ((2 * HD, MINE), F32)],
        scratch=[pltpu.VMEM((2 * HD, MINE), F32)] if last else [],
        flops=COST["attend"],
    )(place, *held, *[c[2] for c in group], *([state] if last else []))[0]


def pair_kernel(which, first, place_ref, own_ref, *refs):
    chunks, refs = refs[: len(which)], refs[len(which) :]
    if not first:
        old_total, refs = refs[0], refs[1:]
    (total,) = refs
    total[...] = jnp.zeros_like(total) if first else old_total[...]
    gap = frame_gap()
    keys_side = lax.broadcasted_iota(jnp.int32, (MINE, 2 * HD), 1) < HD
    own = own_ref[...].astype(F32)
    keys = jnp.where(keys_side, own, 0.0).astype(BF16)
    values = jnp.where(keys_side, 0.0, own).astype(BF16)
    limits = [-chunk_limit(place_ref, back, other) for back, other in which]
    steps = [(i, a) for i in range(len(which)) for a in range(STEPS)]
    turned = {}

    def products(i, a):
        if a == 0:
            turned[i] = flip(chunks[i][:MINE]).astype(BF16)
        count, at = part_of(a)
        return mm(keys[:count], turned[i][:, at]), mm(values[:count], turned[i][:, at])

    ahead = products(*steps[0])
    for n, (i, a) in enumerate(steps):
        scores, grads = ahead
        if n + 1 < len(steps):
            ahead = products(*steps[n + 1])
        if a == 0:
            stats = chunks[i][MINE:].astype(F32)
            log_total, delta = whole_row(stats[: STATS // 2]), whole_row(stats[STATS // 2 :])
        count, at = part_of(a)
        chances = jnp.exp(masked(scores, gap, limits[i]) - log_total[:, at])
        score_grad = (chances * (grads - delta[:, at])).astype(BF16)
        key_grads = mm(score_grad, chunks[i][at])
        value_grads = mm(chances.astype(BF16), chunks[i][at])
        total[:count] += jnp.where(keys_side[:count], key_grads, value_grads)


def pair_pass(step, place, own, group, state=None):
    kernel = functools.partial(pair_kernel, [c[:2] for c in group], state is None)
    return local(
        kernel, f"pair_pass{step}", [((MINE, 2 * HD), F32)], flops=COST["attend"]
    )(place, own, *[c[2] for c in group], *(() if state is None else (state,)))[0]


def output_kernel(
    place_ref, mixed_ref, g0, g1, g2, g3, weight_ref, kept_ref, sent_ref, *share_refs
):
    core, tp = place_ref[1], place_ref[2]
    attention = jnp.concatenate([unfold(mixed_ref[h, :HD]) for h in range(LOCAL)], axis=1)
    for back, ref in enumerate((g0, g1, g2, g3)):
        at = pl.ds(lax.bitwise_and(tp - back, 3) * 2, 2)
        part = mm(ref[...], attention, 0, 0).reshape(2, 4, 2, COLUMNS, WIDTH)
        for y in range(4):
            ours, theirs = part[:, y, 0], part[:, y, 1]
            kept_ref[y, at] = jnp.where(core == 0, ours, theirs).astype(BF16)
            sent_ref[y, at] = jnp.where(core == 0, theirs, ours).astype(BF16)
    for ahead, ref in enumerate(share_refs):
        ref[...] = mm(attention, weight_ref[:, block_of(place_ref, ahead)]).astype(BF16)


def output_side(place, mixed, grads, weight):
    half, share = ((4, LOCAL, COLUMNS, WIDTH), BF16), ((ROWS, WIDTH), BF16)
    call = local(output_kernel, "output_side", [half] * 2 + [share] * TP, flops=COST["small"])
    kept, sent, *shares = call(place, mixed, *grads, weight)
    return kept, sent, shares


def core_sum_kernel(place_ref, kept_ref, got_ref, *out_refs):
    for ahead, ref in enumerate(out_refs):
        y = lax.bitwise_and(place_ref[0] + ahead, 3)
        ref[...] = (kept_ref[y].astype(F32) + got_ref[y].astype(F32)).astype(BF16)


def core_sum(place, kept, got):
    shapes = [((LOCAL, COLUMNS, WIDTH), BF16)] * 4
    return local(core_sum_kernel, "core_sum", shapes)(place, kept, got)


def pack_kernel(pair_ref, query_ref, w0, w1, w2, w3, out_ref):
    out_ref[:, :ROWS] = pair_ref[...].astype(BF16).reshape(LOCAL, ROWS, 2 * HD)
    out_ref[:, ROWS : ROWS + HD] = query_ref[...]
    total = sum(ref[...].astype(F32) for ref in (w0, w1, w2, w3)).astype(BF16)
    for i in range(4):
        at = BACK + COLUMNS * i
        out_ref[:, at : at + COLUMNS] = total[:, :, ROWS * i : ROWS * (i + 1)]


def pack_back(*args):
    shapes = [((LOCAL, BACK + ROWS, 2 * HD), BF16)]
    return local(pack_kernel, "pack_back", shapes, place=False)(*args)[0]


def weight_sum_kernel(back_ref, out_ref):
    for i in range(4):
        at = slice(BACK + COLUMNS * i, BACK + COLUMNS * (i + 1))
        out_ref[:, ROWS * i : ROWS * (i + 1)] = sum(
            back_ref[a, at].astype(F32) for a in range(LOCAL)
        )


def weight_sum(back):
    shapes = [((COLUMNS, WIDTH), F32)]
    return local(weight_sum_kernel, "weight_sum", shapes, place=False)(back)[0]


EXTRA = 16


CUT = 80


def split_line(line):
    high = line.astype(BF16).astype(F32)
    middle = (line - high).astype(BF16).astype(F32)
    rows = [high, middle, line - high - middle, jnp.zeros((EXTRA - 3, line.shape[1]), F32)]
    return jnp.concatenate(rows, axis=0)


def triple_kernel(
    place_ref, back_ref, done_ref, share_ref, weight_ref, triple_ref, line_ref, up_ref, down_ref
):
    pairs = [back_ref[h, :ROWS] for h in range(LOCAL)]
    sides = [
        [unfold(back_ref[h, ROWS:BACK]) for h in range(LOCAL)],
        [pair[:, :HD] for pair in pairs],
        [pair[:, HD:] for pair in pairs],
    ]
    centre = jnp.zeros((ROWS, 1), F32)
    for j in range(3):
        side = jnp.concatenate(sides[j], axis=1)
        triple_ref[j] = side
        both = side.astype(F32) * done_ref[j].astype(F32)
        centre += jnp.sum(both, axis=1, keepdims=True)
    line = jnp.transpose(jnp.broadcast_to(centre, (ROWS, ROWS)))[0:1]
    line = jnp.concatenate([line, jnp.zeros((1, WIDTH - ROWS), F32)], axis=1)
    block = split_line(line).astype(BF16)
    line_ref[...] = block
    far = input_part(place_ref, triple_ref, weight_ref, 2).astype(BF16)
    up_ref[:CUT] = far[:CUT]
    up_ref[CUT:] = share_ref[:HALF]
    down_ref[: ROWS - CUT] = far[CUT:]
    down_ref[ROWS - CUT : REST] = block
    down_ref[REST:] = share_ref[HALF:]


HALF = ROWS // 2
REST = ROWS + EXTRA - CUT


def input_part(place_ref, triple_ref, weight_ref, ahead):
    at = block_of(place_ref, ahead)
    return sum(mm(triple_ref[j], weight_ref[j, at], 1, 1) for j in range(3))


def triple_side(place, back, done, share, weight):
    shapes = [
        ((3, ROWS, WIDTH), BF16),
        ((EXTRA, WIDTH), BF16),
        ((CUT + HALF, WIDTH), BF16),
        ((REST + HALF, WIDTH), BF16),
    ]
    call = local(triple_kernel, "triple_side", shapes, flops=COST["small"])
    return call(place, back, done, share, weight)


def input_kernel(place_ref, triple_ref, weight_ref, near_ref, behind_ref, rest_ref):
    for ahead, ref in ((1, near_ref), (3, behind_ref), (0, rest_ref)):
        ref[...] = input_part(place_ref, triple_ref, weight_ref, ahead)


def input_side(place, triple, weight):
    shapes = [((ROWS, WIDTH), F32)] * 3
    return local(input_kernel, "input_side", shapes, flops=COST["small"])(place, triple, weight)


def merge_kernel(
    near_ref, behind_ref, line_ref, share_near, share_behind, up_ref, down_ref, near_out, behind_out
):
    near_out[:CUT] = (near_ref[:CUT] + up_ref[:CUT].astype(F32)).astype(BF16)
    near_out[CUT:ROWS] = near_ref[CUT:].astype(BF16)
    near_out[ROWS : ROWS + EXTRA] = line_ref[...]
    behind_out[:CUT] = behind_ref[:CUT].astype(BF16)
    behind_out[CUT:ROWS] = (
        behind_ref[CUT:] + down_ref[: ROWS - CUT].astype(F32)
    ).astype(BF16)
    lines = line_ref[...].astype(F32) + down_ref[ROWS - CUT : REST].astype(F32)
    behind_out[ROWS : ROWS + EXTRA] = split_line(
        jnp.sum(lines, axis=0, keepdims=True)
    ).astype(BF16)
    at = ROWS + EXTRA
    near_out[at : at + HALF] = (
        share_near[:HALF].astype(F32) + up_ref[CUT:].astype(F32)
    ).astype(BF16)
    near_out[at + HALF :] = share_near[HALF:]
    behind_out[at : at + HALF] = share_behind[:HALF]
    behind_out[at + HALF :] = (
        share_behind[HALF:].astype(F32) + down_ref[REST:].astype(F32)
    ).astype(BF16)


def merge(*args):
    shapes = [((2 * ROWS + EXTRA, WIDTH), BF16)] * 2
    return local(merge_kernel, "merge", shapes, place=False)(*args)


def finish_kernel(
    rest_ref, line_ref, share_ref, p1, p3, summed_ref, inv_ref, grad_ref, layer_ref, out_ref
):
    total = rest_ref[...] + p1[:ROWS].astype(F32) + p3[:ROWS].astype(F32)
    lines = line_ref[...].astype(F32)
    lines += p1[ROWS : ROWS + EXTRA].astype(F32) + p3[ROWS : ROWS + EXTRA].astype(F32)
    line = jnp.sum(lines[:, :ROWS], axis=0, keepdims=True) / (TP * WIDTH)
    centre = jnp.transpose(jnp.broadcast_to(line, (ROWS, ROWS)))[:, 0:1]
    inv = inv_ref[:, 0:1]
    summed = summed_ref[...].astype(F32)
    out_ref[...] = grad_ref[...].astype(F32) + inv * (total - summed * inv * centre)
    shares = (share_ref[...], p1[ROWS + EXTRA :], p3[ROWS + EXTRA :])
    layer_ref[...] = (summed + sum(share.astype(F32) for share in shares)).astype(BF16)


def finish(*args):
    shapes = [((ROWS, WIDTH), BF16), ((ROWS, WIDTH), F32)]
    return local(finish_kernel, "finish", shapes, place=False)(*args)


def last_ids(code_ids):
    route = [(i, i + 1) for i in range(lax.axis_size(SEQ) - 1)]
    return lax.ppermute(code_ids[:, ROWS - DMAX :], SEQ, route)


def pick_ids(before, code_ids, delays):
    seq_index = lax.axis_index(SEQ)
    joined = jnp.concatenate([before, code_ids], axis=1)
    picked = joined[:, DMAX:]
    for delay in range(1, DMAX + 1):
        moved = joined[:, DMAX - delay : DMAX - delay + ROWS]
        picked = jnp.where(delays[:, None] == delay, moved, picked)
    frames = seq_index * ROWS + jnp.arange(ROWS, dtype=jnp.int32)
    return jnp.where(frames[None, :] >= delays[:, None], picked, -1)[:, :, None]


def over_cores(block):
    return lax.ppermute(block, "core", [(0, 1), (1, 0)])


def body(code_ids, delays, embed_table, project_in, project_out, grad_output):
    place = jnp.stack([lax.axis_index(axis) for axis in ("y", "core", "tp")]).astype(jnp.int32)
    weight_in = project_in.transpose(1, 0, 2)
    up_tp, down_tp = [lambda x, k=k: lax.ppermute(x, "tp", ring(k, TP)) for k in (1, -1)]
    up_y, down_y = [lambda x, k=k: lax.ppermute(x, "y", ring(k, 4)) for k in (1, -1)]
    together = lambda *values: lax.optimization_barrier(values)

    summed = embed(pick_ids(last_ids(code_ids), code_ids, delays), embed_table)
    s1, s3 = up_tp(summed), down_tp(summed)
    summeds = [summed, s1, up_tp(s1), s3]
    grad, _ = together(grad_output, summed)
    g1, g3 = up_tp(grad), down_tp(grad)
    blocks, done, inv = project(place, summeds, weight_in)
    blocks, g1, g3 = together(blocks, g1, g3)
    mine = lax.all_to_all(blocks, HEADS_OVER, 0, 0, tiled=True)

    own, q_columns = prepare(mine)
    g2 = down_tp(g3)
    y1, y3, mate = up_y(own), down_y(own), over_cores(own)
    state = attend(0, place, q_columns, [(0, 0, own), (0, 1, mate)])
    y1, y3, g2, *state = together(y1, y3, g2, *state)
    other1, other3, y2 = over_cores(y1), over_cores(y3), up_y(y1)
    state = attend(1, place, q_columns, [(1, 0, y1), (3, 0, y3)], state)
    y2, *state = together(y2, *state)
    other2 = over_cores(y2)
    state = attend(2, place, q_columns, [(1, 1, other1), (3, 1, other3)], state)
    grads = [grad, g1, g2, g3]
    grad_heads = grad_side(place, grads, project_out)
    mixed, turned, stat = attend(
        3, place, q_columns, [(2, 0, y2), (2, 1, other2)], state, grad_heads
    )
    mixed = lax.all_to_all(mixed, HEADS_OVER, 0, 0, tiled=True)

    both, g_columns, delta = prepare_back(mixed, turned, q_columns, stat)
    held = (q_columns, g_columns, stat, delta)
    b1, b3, b_mate = up_y(both), down_y(both), over_cores(both)
    state = query_pass(
        0, place, held, [(0, 0, own), (0, 1, mate), (1, 0, y1), (1, 1, other1)]
    )
    b1, b3, mixed, state = together(b1, b3, mixed, state)
    b_other1, b_other3, b2 = over_cores(b1), over_cores(b3), up_y(b1)
    kept, sent, shares = output_side(place, mixed, grads, project_out)
    got = over_cores(sent)
    query_grads = query_pass(
        1, place, held, [(2, 0, y2), (2, 1, other2), (3, 0, y3), (3, 1, other3)], state
    )
    query_grads, got, b2, b_mate, b_other1, b_other3 = together(
        query_grads, got, b2, b_mate, b_other1, b_other3
    )
    b_other2 = over_cores(b2)
    w0, w1, w2, w3 = core_sum(place, kept, got)
    w1, w3, w2 = up_y(w1), down_y(w3), up_y(w2)
    own_after, _ = together(own, query_grads)
    state = pair_pass(
        0, place, own_after, [(0, 0, both), (0, 1, b_mate), (1, 0, b1), (3, 0, b3)]
    )
    w1, w2, w3, state = together(w1, w2, w3, state)
    w2 = up_y(w2)
    state = pair_pass(
        1, place, own, [(1, 1, b_other1), (3, 1, b_other3), (2, 0, b2), (2, 1, b_other2)], state
    )
    packed = pack_back(state, query_grads, w0, w1, w2, w3)
    back = lax.all_to_all(packed, HEADS_OVER, 0, 0, tiled=True)

    triple, line, up, down = triple_side(place, back, done, shares[2], weight_in)
    up, down = up_tp(up), down_tp(down)
    near, behind, rest = input_side(place, triple, weight_in)
    near, behind = merge(near, behind, line, shares[1], shares[3], up, down)
    near, behind = up_tp(near), down_tp(behind)
    grad_project_out = weight_sum(back).transpose(1, 0)
    layer_output, grad_embed = finish(
        rest, line, shares[0], near, behind, summed, inv, grad_output
    )
    return layer_output, grad_embed, grad_project_out


def solution(mesh):
    fine = Mesh(mesh.devices.reshape(SPLIT), AXES)
    return jax.shard_map(
        body,
        mesh=fine,
        in_specs=(
            P(None, SEQ),
            P(),
            P(None, None, "tp"),
            P(None, None, "tp"),
            P("tp", None),
            P(SEQ, "tp"),
        ),
        out_specs=(P(SEQ, "tp"), P(SEQ, "tp"), P("tp", SEQ)),
        check_vma=False,
    )
```

```python
import functools

import jax
import jax.numpy as jnp
from jax import lax
from jax.experimental import pallas as pl
from jax.experimental.pallas import tpu as pltpu
from jax.sharding import Mesh, PartitionSpec as P

SPLIT = (2, 4, 4, 2, 4)
AXES = ("zl", "x", "y", "core", "tp")
SEQ = ("zl", "x", "y", "core")
HEADS_OVER = ("zl", "x")

HD = 64
BOOKS = 4
DMAX = 3
VOCAB = 1024
ROWS = 128
WIDTH = 512
LOCAL = 8
TP = 4
COLUMNS = 32
BACK = ROWS + HD
MINE = LOCAL * ROWS
TILE = 256
NEGATIVE = -1e30
EPS = 1e-05
F32 = jnp.float32
BF16 = jnp.bfloat16
MIB = 1024 * 1024
COST = {"small": 4e9, "attend": 5e9}


def mm(left, right, left_axis=1, right_axis=0):
    return lax.dot_general(
        left, right, (((left_axis,), (right_axis,)), ((), ())), preferred_element_type=F32
    )


def ring(distance, count):
    return [(i, (i + distance) % count) for i in range(count)]


def vmem(count):
    return [pl.BlockSpec(memory_space=pltpu.VMEM)] * count


SMEM = pl.BlockSpec(memory_space=pltpu.SMEM)


def local(kernel, name, shapes, scratch=(), flops=0, place=True):
    def call(*args):
        outs = [jax.ShapeDtypeStruct(shape, kind) for shape, kind in shapes]
        moved = sum(a.size * a.dtype.itemsize for a in (*args, *outs))
        return pl.pallas_call(
            kernel,
            in_specs=([SMEM] if place else []) + vmem(len(args) - place),
            out_specs=vmem(len(outs)),
            out_shape=outs,
            scratch_shapes=list(scratch),
            compiler_params=pltpu.CompilerParams(vmem_limit_bytes=16 * MIB),
            cost_estimate=pl.CostEstimate(flops=int(flops), transcendentals=0, bytes_accessed=moved),
            name=name,
        )(*args)

    return call


def block_of(place_ref, step):
    return pl.ds(pl.multiple_of(lax.bitwise_and(place_ref[2] + step, 3) * WIDTH, WIDTH), WIDTH)


def fold(rows):
    return jnp.concatenate([rows[:HD], rows[HD:]], axis=1)


def unfold(folded):
    return jnp.concatenate([folded[:, :HD], folded[:, HD:]], axis=0)


def embed_kernel(place_ref, before_ref, ids_ref, table_ref, out_ref):
    before, ids = before_ref[...], ids_ref[...]
    moved = [ids] + [
        jnp.concatenate([before[:, DMAX - d :], ids[:, : ROWS - d]], axis=1)
        for d in range(1, DMAX + 1)
    ]
    frames = place_ref[3] + lax.broadcasted_iota(jnp.int32, (1, ROWS), 1)
    rows = []
    for book in range(BOOKS):
        delay, row = place_ref[4 + book], moved[0][book : book + 1]
        for d in range(1, DMAX + 1):
            row = jnp.where(delay == d, moved[d][book : book + 1], row)
        rows.append(jnp.where(frames >= delay, row, -1).astype(F32))
    columns = jnp.transpose(jnp.concatenate(rows * 2, axis=0)).astype(jnp.int32)
    entries = lax.broadcasted_iota(jnp.int32, (ROWS, VOCAB), 1)
    total = jnp.zeros((ROWS, WIDTH), F32)
    for book in range(BOOKS):
        chosen = jnp.where(entries == columns[:, book : book + 1], 1.0, 0.0).astype(BF16)
        total += mm(chosen, table_ref[book])
    out_ref[...] = total.astype(BF16)


def embed(place, before, ids, table):
    return local(embed_kernel, "embed", [((ROWS, WIDTH), BF16)])(place, before, ids, table)[0]


def grad_side_kernel(place_ref, g0, g1, g2, g3, weight_ref, out_ref):
    total = jnp.zeros((ROWS, WIDTH), F32)
    for back, ref in enumerate((g0, g1, g2, g3)):
        total += mm(ref[...], weight_ref[:, block_of(place_ref, -back)], 1, 1)
    for h in range(LOCAL):
        out_ref[h] = fold(total[:, h * HD : (h + 1) * HD]).astype(BF16)


def grad_side(place, grads, weight):
    call = local(grad_side_kernel, "grad_side", [((LOCAL, HD, 2 * HD), BF16)], flops=COST["small"])
    return call(place, *grads, weight)[0]


def project_kernel(place_ref, s0, s1, s2, s3, weight_ref, out_ref, done_ref, inv_ref):
    parts = [ref[...].astype(F32) for ref in (s0, s1, s2, s3)]
    squares = sum(jnp.sum(part * part, axis=1, keepdims=True) for part in parts)
    inv = lax.rsqrt(squares / (TP * WIDTH) + EPS)
    inv_ref[...] = jnp.broadcast_to(inv, (ROWS, 128))
    normed = [(part * inv).astype(BF16) for part in parts]
    done = []
    for j in range(3):
        total = jnp.zeros((ROWS, WIDTH), F32)
        for back in range(TP):
            total += mm(normed[back], weight_ref[j, block_of(place_ref, -back)])
        done.append(total.astype(BF16))
        done_ref[j] = done[j]
    for h in range(LOCAL):
        q, k, v = [part[:, h * HD : (h + 1) * HD] for part in done]
        out_ref[h, :ROWS] = jnp.concatenate([k, v], axis=1)
        out_ref[h, ROWS:] = fold(q)


def project(place, summeds, weight):
    shapes = [
        ((LOCAL, BACK, 2 * HD), BF16),
        ((3, ROWS, WIDTH), BF16),
        ((ROWS, 128), F32),
    ]
    call = local(project_kernel, "project", shapes, flops=COST["small"])
    return call(place, *summeds, weight)


def flip(block):
    return jnp.transpose(block.astype(F32))


def frame_gap():
    keys = lax.broadcasted_iota(jnp.int32, (TILE, TILE), 0)
    queries = lax.broadcasted_iota(jnp.int32, (TILE, TILE), 1)
    frame = lambda i: lax.shift_right_logical(i, 7) * (LOCAL * ROWS) + lax.bitwise_and(i, ROWS - 1)
    return frame(keys) - frame(queries)


def chunk_limit(place_ref, back, other):
    y, core = place_ref[0], place_ref[1]
    chunk = lax.bitwise_and(y - back, 3) * 2 + (1 - core if other else core)
    return (2 * y + core - chunk) * ROWS


STEPS = MINE // TILE


def part_of(a):
    return TILE * (a + 1), slice(TILE * a, TILE * (a + 1))


def masked(scores, gap, limit):
    last = jnp.where(gap <= limit, scores[scores.shape[0] - TILE :], NEGATIVE)
    if scores.shape[0] == TILE:
        return last
    return jnp.concatenate([scores[: scores.shape[0] - TILE], last], axis=0)


def pack(rows):
    halves = rows.reshape(LOCAL, 2, HD, HD)
    return jnp.concatenate([halves[:, 0], halves[:, 1]], axis=2)


def prepare_kernel(mine_ref, pair_ref, columns_ref):
    queries = [unfold(mine_ref[a, ROWS:]).astype(F32) for a in range(LOCAL)]
    queries = jnp.concatenate(queries, axis=0) * (HD**-0.5)
    wide = jnp.concatenate([queries, jnp.zeros((MINE, HD), F32)], axis=1)
    columns_ref[...] = jnp.transpose(wide).astype(BF16)
    for a in range(LOCAL):
        pair_ref[a * ROWS : (a + 1) * ROWS] = mine_ref[a, :ROWS]


def prepare(mine):
    shapes = [((MINE, 2 * HD), BF16), ((2 * HD, MINE), BF16)]
    return local(prepare_kernel, "prepare", shapes, place=False)(mine)


STATS = 48


def three_parts(row):
    block = jnp.concatenate([row[:, i * ROWS : (i + 1) * ROWS] for i in range(LOCAL)], axis=0)
    high = block.astype(BF16).astype(F32)
    middle = (block - high).astype(BF16).astype(F32)
    return jnp.concatenate([high, middle, block - high - middle], axis=0)


def whole_row(parts):
    block = parts[:LOCAL] + parts[LOCAL : 2 * LOCAL] + parts[2 * LOCAL :]
    return jnp.concatenate([block[i : i + 1] for i in range(LOCAL)], axis=1)


def prepare_back_kernel(mixed_ref, turned_ref, q_columns, stat_ref, both_ref, columns_ref, delta_ref):
    grads = [unfold(mixed_ref[a, HD:]).astype(F32) for a in range(LOCAL)]
    grads = jnp.concatenate(grads, axis=0)
    queries = jnp.transpose(q_columns[...].astype(F32))
    columns = jnp.transpose(jnp.concatenate([jnp.zeros((MINE, HD), F32), grads], axis=1))
    columns_ref[...] = columns.astype(BF16)
    both = columns[HD:] * turned_ref[...].astype(F32)
    delta = jnp.sum(both, axis=0, keepdims=True)
    delta_ref[...] = jnp.broadcast_to(delta, (8, MINE))
    both_ref[:MINE] = jnp.concatenate([queries[:, :HD], grads], axis=1).astype(BF16)
    stats = jnp.concatenate([three_parts(stat_ref[0:1]), three_parts(delta)], axis=0)
    both_ref[MINE:] = stats.astype(BF16)


def prepare_back(*args):
    shapes = [((MINE + STATS, 2 * HD), BF16), ((2 * HD, MINE), BF16), ((8, MINE), F32)]
    return local(prepare_back_kernel, "prepare_back", shapes, place=False)(*args)


def forward_kernel(which, first, last, place_ref, columns_ref, *refs):
    chunks, refs = refs[:2], refs[2:]
    if not first:
        (old_total, old_top), refs = refs[:2], refs[2:]
    if last:
        grad_ref, out_ref, turned_ref, stat_ref, total, top = refs
    else:
        total, top = refs
    if first:
        total[...] = jnp.zeros_like(total)
        top[...] = jnp.full_like(top, NEGATIVE)
    else:
        total[...] = old_total[...]
        top[...] = old_top[...]
    feature = lax.broadcasted_iota(jnp.int32, (2 * HD, MINE), 0)
    gap = frame_gap()
    limits = [chunk_limit(place_ref, back, other) for back, other in which]
    values = [jnp.where(feature < HD, 1.0, flip(ref[...])).astype(BF16) for ref in chunks]

    def scores_of(a):
        count, at = part_of(a)
        return [
            masked(mm(ref[:count], columns_ref[:, at]), gap, limit)
            for ref, limit in zip(chunks, limits, strict=True)
        ]

    scores = scores_of(0)
    for a in range(STEPS):
        now, scores = scores, scores_of(a + 1) if a + 1 < STEPS else None
        count, at = part_of(a)
        old = top[0:1, at]
        new = old
        for score in now:
            new = jnp.maximum(new, jnp.max(score, axis=0, keepdims=True))
        added = total[:, at] * jnp.exp(old - new)
        for score, value in zip(now, values, strict=True):
            added += mm(value[:, :count], jnp.exp(score - new).astype(BF16))
        total[:, at] = added
        top[0:1, at] = new
    if last:
        row_total = total[0:1]
        attended = (total[HD:] / row_total).astype(BF16).astype(F32)
        stat_ref[...] = jnp.broadcast_to(top[0:1] + jnp.log(row_total), (8, MINE))
        turned_ref[...] = attended.astype(BF16)
        out_ref[:, :HD] = pack(jnp.transpose(attended)).astype(BF16)
        out_ref[:, HD:] = grad_ref[...]


def attend(step, place, columns, group, state=(), grads=None):
    held = [((2 * HD, MINE), F32), ((8, MINE), F32)]
    last = grads is not None
    outs = [((LOCAL, ROWS, 2 * HD), BF16), ((HD, MINE), BF16), ((8, MINE), F32)]
    kernel = functools.partial(forward_kernel, [c[:2] for c in group], not state, last)
    return local(
        kernel,
        f"attend{step}",
        outs if last else held,
        scratch=[pltpu.VMEM(*h) for h in held] if last else [],
        flops=COST["attend"],
    )(place, columns, *[c[2] for c in group], *state, *([grads] if last else []))


def query_visits(which, place_ref, held, chunks, total):
    q_columns, g_columns, stat_ref, delta_ref = held
    gap = frame_gap()
    limits = [chunk_limit(place_ref, back, other) for back, other in which]
    steps = [(i, a) for i in range(len(which)) for a in range(STEPS)]

    def products(i, a):
        count, at = part_of(a)
        pair = chunks[i][:count]
        return mm(pair, q_columns[:, at]), mm(pair, g_columns[:, at])

    ahead = products(*steps[0])
    for n, (i, a) in enumerate(steps):
        scores, grads = ahead
        if n + 1 < len(steps):
            ahead = products(*steps[n + 1])
        if a == 0:
            turned = flip(chunks[i][...]).astype(BF16)
        count, at = part_of(a)
        chances = jnp.exp(masked(scores, gap, limits[i]) - stat_ref[0:1, at])
        score_grad = (chances * (grads - delta_ref[0:1, at])).astype(BF16)
        total[:, at] += mm(turned[:, :count], score_grad)


def pair_visits(which, place_ref, own_ref, chunks, total):
    gap = frame_gap()
    keys_side = lax.broadcasted_iota(jnp.int32, (MINE, 2 * HD), 1) < HD
    own = own_ref[...].astype(F32)
    keys = jnp.where(keys_side, own, 0.0).astype(BF16)
    values = jnp.where(keys_side, 0.0, own).astype(BF16)
    limits = [-chunk_limit(place_ref, back, other) for back, other in which]
    steps = [(i, a) for i in range(len(which)) for a in range(STEPS)]
    turned = {}

    def products(i, a):
        if a == 0:
            turned[i] = flip(chunks[i][:MINE]).astype(BF16)
        count, at = part_of(a)
        return mm(keys[:count], turned[i][:, at]), mm(values[:count], turned[i][:, at])

    ahead = products(*steps[0])
    for n, (i, a) in enumerate(steps):
        scores, grads = ahead
        if n + 1 < len(steps):
            ahead = products(*steps[n + 1])
        if a == 0:
            stats = chunks[i][MINE:].astype(F32)
            log_total, delta = whole_row(stats[: STATS // 2]), whole_row(stats[STATS // 2 :])
        count, at = part_of(a)
        chances = jnp.exp(masked(scores, gap, limits[i]) - log_total[:, at])
        score_grad = (chances * (grads - delta[:, at])).astype(BF16)
        key_grads = mm(score_grad, chunks[i][at])
        value_grads = mm(chances.astype(BF16), chunks[i][at])
        total[:count] += jnp.where(keys_side[:count], key_grads, value_grads)


QUERY_TOTAL = ((2 * HD, MINE), F32)
PAIR_TOTAL = ((MINE, 2 * HD), F32)


def query_kernel(which, place_ref, *refs):
    held, (*chunks, total) = refs[:4], refs[4:]
    total[...] = jnp.zeros_like(total)
    query_visits(which, place_ref, held, chunks, total)


def query_pass(place, held, group):
    kernel = functools.partial(query_kernel, [c[:2] for c in group])
    call = local(kernel, "query_pass", [QUERY_TOTAL], flops=COST["attend"])
    return call(place, *held, *[c[2] for c in group])[0]


def both_kernel(which, pair_which, place_ref, *refs):
    held, refs = refs[:4], refs[4:]
    chunks, refs = refs[: len(which)], refs[len(which) :]
    query_chunks, refs = refs[: len(pair_which)], refs[len(pair_which) :]
    own_ref, old_total, out_ref, pair_total, total = refs
    total[...] = old_total[...]
    query_visits(which, place_ref, held, chunks, total)
    out_ref[...] = pack(jnp.transpose(total[:HD] * (HD**-0.5))).astype(BF16)
    pair_total[...] = jnp.zeros_like(pair_total)
    pair_visits(pair_which, place_ref, own_ref, query_chunks, pair_total)


def both_pass(place, held, group, pair_group, own, state):
    kernel = functools.partial(both_kernel, [c[:2] for c in group], [c[:2] for c in pair_group])
    call = local(
        kernel, "both_pass", [((LOCAL, HD, 2 * HD), BF16), PAIR_TOTAL],
        scratch=[pltpu.VMEM(*QUERY_TOTAL)], flops=2 * COST["attend"],
    )
    return call(place, *held, *[c[2] for c in group + pair_group], own, state)


def pair_kernel(which, place_ref, own_ref, *refs):
    *chunks, old_total, total = refs
    total[...] = old_total[...]
    pair_visits(which, place_ref, own_ref, chunks, total)


def pair_pass(step, place, own, group, state):
    kernel = functools.partial(pair_kernel, [c[:2] for c in group])
    call = local(kernel, f"pair_pass{step}", [PAIR_TOTAL], flops=COST["attend"])
    return call(place, own, *[c[2] for c in group], state)[0]


def output_kernel(
    place_ref, mixed_ref, g0, g1, g2, g3, weight_ref, kept_ref, sent_ref, *share_refs
):
    core, tp = place_ref[1], place_ref[2]
    attention = jnp.concatenate([unfold(mixed_ref[h, :HD]) for h in range(LOCAL)], axis=1)
    for back, ref in enumerate((g0, g1, g2, g3)):
        at = pl.ds(lax.bitwise_and(tp - back, 3) * 2, 2)
        part = mm(ref[...], attention, 0, 0).reshape(2, 4, 2, COLUMNS, WIDTH)
        for y in range(4):
            ours, theirs = part[:, y, 0], part[:, y, 1]
            kept_ref[y, at] = jnp.where(core == 0, ours, theirs).astype(BF16)
            sent_ref[y, at] = jnp.where(core == 0, theirs, ours).astype(BF16)
    for ahead, ref in enumerate(share_refs):
        ref[...] = mm(attention, weight_ref[:, block_of(place_ref, ahead)]).astype(BF16)


def output_side(place, mixed, grads, weight):
    half, share = ((4, LOCAL, COLUMNS, WIDTH), BF16), ((ROWS, WIDTH), BF16)
    call = local(output_kernel, "output_side", [half] * 2 + [share] * TP, flops=COST["small"])
    kept, sent, *shares = call(place, mixed, *grads, weight)
    return kept, sent, shares


def core_sum_kernel(place_ref, kept_ref, got_ref, *out_refs):
    for ahead, ref in enumerate(out_refs):
        y = lax.bitwise_and(place_ref[0] + ahead, 3)
        ref[...] = (kept_ref[y].astype(F32) + got_ref[y].astype(F32)).astype(BF16)


def core_sum(place, kept, got):
    shapes = [((LOCAL, COLUMNS, WIDTH), BF16)] * 4
    return local(core_sum_kernel, "core_sum", shapes)(place, kept, got)


def add_kernel(left_ref, right_ref, out_ref):
    out_ref[...] = (left_ref[...].astype(F32) + right_ref[...].astype(F32)).astype(BF16)


def add(left, right):
    return local(add_kernel, "add", [(left.shape, BF16)], place=False)(left, right)[0]


def pack_kernel(pair_ref, query_ref, w0, w1, w3, out_ref):
    out_ref[:, :ROWS] = pair_ref[...].astype(BF16).reshape(LOCAL, ROWS, 2 * HD)
    out_ref[:, ROWS : ROWS + HD] = query_ref[...]
    total = sum(ref[...].astype(F32) for ref in (w0, w1, w3)).astype(BF16)
    for i in range(4):
        at = BACK + COLUMNS * i
        out_ref[:, at : at + COLUMNS] = total[:, :, ROWS * i : ROWS * (i + 1)]


def pack_back(*args):
    shapes = [((LOCAL, BACK + ROWS, 2 * HD), BF16)]
    return local(pack_kernel, "pack_back", shapes, place=False)(*args)[0]


def weight_sum_kernel(back_ref, out_ref):
    for i in range(4):
        at = slice(BACK + COLUMNS * i, BACK + COLUMNS * (i + 1))
        out_ref[:, ROWS * i : ROWS * (i + 1)] = sum(
            back_ref[a, at].astype(F32) for a in range(LOCAL)
        )


def weight_sum(back):
    shapes = [((COLUMNS, WIDTH), F32)]
    return local(weight_sum_kernel, "weight_sum", shapes, place=False)(back)[0]


EXTRA = 16


CUT = 80


def split_line(line):
    high = line.astype(BF16).astype(F32)
    middle = (line - high).astype(BF16).astype(F32)
    rows = [high, middle, line - high - middle, jnp.zeros((EXTRA - 3, line.shape[1]), F32)]
    return jnp.concatenate(rows, axis=0)


def triple_kernel(
    place_ref, back_ref, done_ref, share_ref, weight_ref, triple_ref, line_ref, up_ref, down_ref
):
    pairs = [back_ref[h, :ROWS] for h in range(LOCAL)]
    sides = [
        [unfold(back_ref[h, ROWS:BACK]) for h in range(LOCAL)],
        [pair[:, :HD] for pair in pairs],
        [pair[:, HD:] for pair in pairs],
    ]
    centre = jnp.zeros((ROWS, 1), F32)
    for j in range(3):
        side = jnp.concatenate(sides[j], axis=1)
        triple_ref[j] = side
        both = side.astype(F32) * done_ref[j].astype(F32)
        centre += jnp.sum(both, axis=1, keepdims=True)
    line = jnp.transpose(jnp.broadcast_to(centre, (ROWS, ROWS)))[0:1]
    line = jnp.concatenate([line, jnp.zeros((1, WIDTH - ROWS), F32)], axis=1)
    block = split_line(line).astype(BF16)
    line_ref[...] = block
    far = input_part(place_ref, triple_ref, weight_ref, 2).astype(BF16)
    up_ref[:CUT] = far[:CUT]
    up_ref[CUT:] = share_ref[:HALF]
    down_ref[: ROWS - CUT] = far[CUT:]
    down_ref[ROWS - CUT : REST] = block
    down_ref[REST:] = share_ref[HALF:]


HALF = ROWS // 2
REST = ROWS + EXTRA - CUT


def input_part(place_ref, triple_ref, weight_ref, ahead):
    at = block_of(place_ref, ahead)
    return sum(mm(triple_ref[j], weight_ref[j, at], 1, 1) for j in range(3))


def triple_side(place, back, done, share, weight):
    shapes = [
        ((3, ROWS, WIDTH), BF16),
        ((EXTRA, WIDTH), BF16),
        ((CUT + HALF, WIDTH), BF16),
        ((REST + HALF, WIDTH), BF16),
    ]
    call = local(triple_kernel, "triple_side", shapes, flops=COST["small"])
    return call(place, back, done, share, weight)


def input_kernel(place_ref, triple_ref, weight_ref, near_ref, behind_ref, rest_ref):
    for ahead, ref in ((1, near_ref), (3, behind_ref), (0, rest_ref)):
        ref[...] = input_part(place_ref, triple_ref, weight_ref, ahead)


def input_side(place, triple, weight):
    shapes = [((ROWS, WIDTH), F32)] * 3
    return local(input_kernel, "input_side", shapes, flops=COST["small"])(place, triple, weight)


def merge_kernel(
    near_ref, behind_ref, line_ref, share_near, share_behind, up_ref, down_ref, near_out, behind_out
):
    near_out[:CUT] = (near_ref[:CUT] + up_ref[:CUT].astype(F32)).astype(BF16)
    near_out[CUT:ROWS] = near_ref[CUT:].astype(BF16)
    near_out[ROWS : ROWS + EXTRA] = line_ref[...]
    behind_out[:CUT] = behind_ref[:CUT].astype(BF16)
    behind_out[CUT:ROWS] = (
        behind_ref[CUT:] + down_ref[: ROWS - CUT].astype(F32)
    ).astype(BF16)
    lines = line_ref[...].astype(F32) + down_ref[ROWS - CUT : REST].astype(F32)
    behind_out[ROWS : ROWS + EXTRA] = split_line(
        jnp.sum(lines, axis=0, keepdims=True)
    ).astype(BF16)
    at = ROWS + EXTRA
    near_out[at : at + HALF] = (
        share_near[:HALF].astype(F32) + up_ref[CUT:].astype(F32)
    ).astype(BF16)
    near_out[at + HALF :] = share_near[HALF:]
    behind_out[at : at + HALF] = share_behind[:HALF]
    behind_out[at + HALF :] = (
        share_behind[HALF:].astype(F32) + down_ref[REST:].astype(F32)
    ).astype(BF16)


def merge(*args):
    shapes = [((2 * ROWS + EXTRA, WIDTH), BF16)] * 2
    return local(merge_kernel, "merge", shapes, place=False)(*args)


def finish_kernel(
    rest_ref, line_ref, share_ref, p1, p3, summed_ref, inv_ref, grad_ref, layer_ref, out_ref
):
    total = rest_ref[...] + p1[:ROWS].astype(F32) + p3[:ROWS].astype(F32)
    lines = line_ref[...].astype(F32)
    lines += p1[ROWS : ROWS + EXTRA].astype(F32) + p3[ROWS : ROWS + EXTRA].astype(F32)
    line = jnp.sum(lines[:, :ROWS], axis=0, keepdims=True) / (TP * WIDTH)
    centre = jnp.transpose(jnp.broadcast_to(line, (ROWS, ROWS)))[:, 0:1]
    inv = inv_ref[:, 0:1]
    summed = summed_ref[...].astype(F32)
    out_ref[...] = grad_ref[...].astype(F32) + inv * (total - summed * inv * centre)
    shares = (share_ref[...], p1[ROWS + EXTRA :], p3[ROWS + EXTRA :])
    layer_ref[...] = (summed + sum(share.astype(F32) for share in shares)).astype(BF16)


def finish(*args):
    shapes = [((ROWS, WIDTH), BF16), ((ROWS, WIDTH), F32)]
    return local(finish_kernel, "finish", shapes, place=False)(*args)


def last_ids(code_ids):
    route = [(i, i + 1) for i in range(lax.axis_size(SEQ) - 1)]
    return lax.ppermute(code_ids[:, ROWS - DMAX :], SEQ, route)


def over_cores(block):
    return lax.ppermute(block, "core", [(0, 1), (1, 0)])


def body(code_ids, delays, embed_table, project_in, project_out, grad_output):
    place = [lax.axis_index(axis) for axis in ("y", "core", "tp")]
    place = jnp.stack(place + [lax.axis_index(SEQ) * ROWS]).astype(jnp.int32)
    place = jnp.concatenate([place, delays])
    weight_in = project_in.transpose(1, 0, 2)
    up_tp, down_tp = [lambda x, k=k: lax.ppermute(x, "tp", ring(k, TP)) for k in (1, -1)]
    up_y, down_y = [lambda x, k=k: lax.ppermute(x, "y", ring(k, 4)) for k in (1, -1)]
    together = lambda *values: lax.optimization_barrier(values)

    summed = embed(place, last_ids(code_ids), code_ids, embed_table)
    s1, s3 = up_tp(summed), down_tp(summed)
    summeds = [summed, s1, up_tp(s1), s3]
    grad, _ = together(grad_output, summed)
    g1, g3 = up_tp(grad), down_tp(grad)
    blocks, done, inv = project(place, summeds, weight_in)
    blocks, g1, g3 = together(blocks, g1, g3)
    mine = lax.all_to_all(blocks, HEADS_OVER, 0, 0, tiled=True)

    own, q_columns = prepare(mine)
    g2 = down_tp(g3)
    y1, y3, mate = up_y(own), down_y(own), over_cores(own)
    state = attend(0, place, q_columns, [(0, 0, own), (0, 1, mate)])
    y1, y3, g2, *state = together(y1, y3, g2, *state)
    other1, other3, y2 = over_cores(y1), over_cores(y3), up_y(y1)
    state = attend(1, place, q_columns, [(1, 0, y1), (3, 0, y3)], state)
    y2, *state = together(y2, *state)
    other2 = over_cores(y2)
    state = attend(2, place, q_columns, [(1, 1, other1), (3, 1, other3)], state)
    grads = [grad, g1, g2, g3]
    grad_heads = grad_side(place, grads, project_out)
    mixed, turned, stat = attend(
        3, place, q_columns, [(2, 0, y2), (2, 1, other2)], state, grad_heads
    )
    mixed = lax.all_to_all(mixed, HEADS_OVER, 0, 0, tiled=True)

    both, g_columns, delta = prepare_back(mixed, turned, q_columns, stat)
    held = (q_columns, g_columns, stat, delta)
    kept, sent, shares = output_side(place, mixed, grads, project_out)
    b1, b3, b_mate, got = up_y(both), down_y(both), over_cores(both), over_cores(sent)
    state = query_pass(place, held, [(0, 0, own), (0, 1, mate), (1, 0, y1), (1, 1, other1)])
    b1, b3, b_mate, got, state = together(b1, b3, b_mate, got, state)
    w0, w1, w2, w3 = core_sum(place, kept, got)
    w2, w3, b2 = up_y(w2), down_y(w3), up_y(b1)
    b_other1, b_other3 = over_cores(b1), over_cores(b3)
    query_grads, state = both_pass(
        place,
        held,
        [(2, 0, y2), (2, 1, other2), (3, 0, y3), (3, 1, other3)],
        [(0, 0, both), (0, 1, b_mate)],
        own,
        state,
    )
    w2, w3, b2, b_other1, b_other3, state = together(w2, w3, b2, b_other1, b_other3, state)
    w1, b_other2 = up_y(add(w1, w2)), over_cores(b2)
    state = pair_pass(
        0, place, own, [(1, 0, b1), (3, 0, b3), (1, 1, b_other1), (3, 1, b_other3)], state
    )
    w1, b_other2, state = together(w1, b_other2, state)
    state = pair_pass(1, place, own, [(2, 0, b2), (2, 1, b_other2)], state)
    packed = pack_back(state, query_grads, w0, w1, w3)
    back = lax.all_to_all(packed, HEADS_OVER, 0, 0, tiled=True)

    triple, line, up, down = triple_side(place, back, done, shares[2], weight_in)
    up, down = up_tp(up), down_tp(down)
    near, behind, rest = input_side(place, triple, weight_in)
    near, behind = merge(near, behind, line, shares[1], shares[3], up, down)
    near, behind = up_tp(near), down_tp(behind)
    grad_project_out = weight_sum(back).transpose(1, 0)
    layer_output, grad_embed = finish(
        rest, line, shares[0], near, behind, summed, inv, grad_output
    )
    return layer_output, grad_embed, grad_project_out


def solution(mesh):
    fine = Mesh(mesh.devices.reshape(SPLIT), AXES)
    return jax.shard_map(
        body,
        mesh=fine,
        in_specs=(
            P(None, SEQ),
            P(),
            P(None, None, "tp"),
            P(None, None, "tp"),
            P("tp", None),
            P(SEQ, "tp"),
        ),
        out_specs=(P(SEQ, "tp"), P(SEQ, "tp"), P("tp", SEQ)),
        check_vma=False,
    )
```

```python
import functools

import jax
import jax.numpy as jnp
from jax import lax
from jax.experimental import pallas as pl
from jax.experimental.pallas import tpu as pltpu
from jax.sharding import Mesh, PartitionSpec as P

SPLIT = (2, 4, 4, 2, 4)
AXES = ("zl", "x", "y", "core", "tp")
SEQ = ("zl", "x", "y", "core")
HEADS_OVER = ("zl", "x")

HD = 64
BOOKS = 4
DMAX = 3
VOCAB = 1024
ROWS = 128
WIDTH = 512
LOCAL = 8
TP = 4
COLUMNS = 32
BACK = ROWS + HD
MINE = LOCAL * ROWS
TILE = 256
NEGATIVE = -1e30
EPS = 1e-05
F32 = jnp.float32
BF16 = jnp.bfloat16
MIB = 1024 * 1024
COST = {"small": 4e9, "attend": 5e9}


def mm(left, right, left_axis=1, right_axis=0):
    return lax.dot_general(
        left, right, (((left_axis,), (right_axis,)), ((), ())), preferred_element_type=F32
    )


def ring(distance, count):
    return [(i, (i + distance) % count) for i in range(count)]


def vmem(count):
    return [pl.BlockSpec(memory_space=pltpu.VMEM)] * count


SMEM = pl.BlockSpec(memory_space=pltpu.SMEM)


def local(kernel, name, shapes, scratch=(), flops=0, place=True):
    def call(*args):
        outs = [jax.ShapeDtypeStruct(shape, kind) for shape, kind in shapes]
        moved = sum(a.size * a.dtype.itemsize for a in (*args, *outs))
        return pl.pallas_call(
            kernel,
            in_specs=([SMEM] if place else []) + vmem(len(args) - place),
            out_specs=vmem(len(outs)),
            out_shape=outs,
            scratch_shapes=list(scratch),
            compiler_params=pltpu.CompilerParams(vmem_limit_bytes=16 * MIB),
            cost_estimate=pl.CostEstimate(flops=int(flops), transcendentals=0, bytes_accessed=moved),
            name=name,
        )(*args)

    return call


def block_of(place_ref, step):
    return pl.ds(pl.multiple_of(lax.bitwise_and(place_ref[2] + step, 3) * WIDTH, WIDTH), WIDTH)


def fold(rows):
    return jnp.concatenate([rows[:HD], rows[HD:]], axis=1)


def unfold(folded):
    return jnp.concatenate([folded[:, :HD], folded[:, HD:]], axis=0)


def embed_kernel(place_ref, before_ref, ids_ref, table_ref, out_ref):
    before, ids = before_ref[...], ids_ref[...]
    moved = [ids] + [
        jnp.concatenate([before[:, ROWS - d :], ids[:, : ROWS - d]], axis=1)
        for d in range(1, DMAX + 1)
    ]
    frames = place_ref[3] + lax.broadcasted_iota(jnp.int32, (1, ROWS), 1)
    rows = []
    for book in range(BOOKS):
        delay, row = place_ref[4 + book], moved[0][book : book + 1]
        for d in range(1, DMAX + 1):
            row = jnp.where(delay == d, moved[d][book : book + 1], row)
        rows.append(jnp.where(frames >= delay, row, -1).astype(F32))
    columns = jnp.transpose(jnp.concatenate(rows * 2, axis=0)).astype(jnp.int32)
    entries = lax.broadcasted_iota(jnp.int32, (ROWS, VOCAB), 1)
    total = jnp.zeros((ROWS, WIDTH), F32)
    for book in range(BOOKS):
        chosen = jnp.where(entries == columns[:, book : book + 1], 1.0, 0.0).astype(BF16)
        total += mm(chosen, table_ref[book])
    out_ref[...] = total.astype(BF16)


def embed(place, before, ids, table):
    return local(embed_kernel, "embed", [((ROWS, WIDTH), BF16)])(place, before, ids, table)[0]


def grad_side_kernel(place_ref, g0, g1, g2, g3, weight_ref, out_ref):
    total = jnp.zeros((ROWS, WIDTH), F32)
    for back, ref in enumerate((g0, g1, g2, g3)):
        total += mm(ref[...], weight_ref[:, block_of(place_ref, -back)], 1, 1)
    for h in range(LOCAL):
        out_ref[h] = fold(total[:, h * HD : (h + 1) * HD]).astype(BF16)


def grad_side(place, grads, weight):
    call = local(grad_side_kernel, "grad_side", [((LOCAL, HD, 2 * HD), BF16)], flops=COST["small"])
    return call(place, *grads, weight)[0]


def project_start_kernel(place_ref, s0, s1, s3, weight_ref, total_ref, squares_ref, rest_ref):
    squares = jnp.zeros((ROWS, 1), F32)
    totals = [jnp.zeros((ROWS, WIDTH), F32)] * 3
    for back, ref in ((0, s0), (1, s1), (3, s3)):
        part = ref[...].astype(F32)
        squares += jnp.sum(part * part, axis=1, keepdims=True)
        for j in range(3):
            totals[j] += mm(ref[...], weight_ref[j, block_of(place_ref, -back)])
    for j in range(3):
        total_ref[j] = totals[j]
        rest_ref[j] = weight_ref[j, block_of(place_ref, -2)]
    squares_ref[...] = jnp.broadcast_to(squares, (ROWS, 128))


def project_kernel(s2, rest_ref, total_ref, squares_ref, out_ref, done_ref, inv_ref):
    part = s2[...].astype(F32)
    squares = squares_ref[:, 0:1] + jnp.sum(part * part, axis=1, keepdims=True)
    inv = lax.rsqrt(squares / (TP * WIDTH) + EPS)
    inv_ref[...] = jnp.broadcast_to(inv, (ROWS, 128))
    done = []
    for j in range(3):
        done.append(((total_ref[j] + mm(s2[...], rest_ref[j])) * inv).astype(BF16))
        done_ref[j] = done[j]
    for h in range(LOCAL):
        q, k, v = [part[:, h * HD : (h + 1) * HD] for part in done]
        out_ref[h, :ROWS] = jnp.concatenate([k, v], axis=1)
        out_ref[h, ROWS:] = fold(q)


def project(place, summeds, weight):
    s0, s1, s2, s3 = summeds
    shapes = [((3, ROWS, WIDTH), F32), ((ROWS, 128), F32), ((3, WIDTH, WIDTH), BF16)]
    call = local(project_start_kernel, "project_start", shapes, flops=COST["small"])
    total, squares, rest = call(place, s0, s1, s3, weight)
    shapes = [
        ((LOCAL, BACK, 2 * HD), BF16),
        ((3, ROWS, WIDTH), BF16),
        ((ROWS, 128), F32),
    ]
    call = local(project_kernel, "project", shapes, flops=COST["small"], place=False)
    return call(s2, rest, total, squares)


def flip(block):
    return jnp.transpose(block.astype(F32))


def frame_gap():
    keys = lax.broadcasted_iota(jnp.int32, (TILE, TILE), 0)
    queries = lax.broadcasted_iota(jnp.int32, (TILE, TILE), 1)
    frame = lambda i: lax.shift_right_logical(i, 7) * (LOCAL * ROWS) + lax.bitwise_and(i, ROWS - 1)
    return frame(keys) - frame(queries)


def chunk_limit(place_ref, back, other):
    y, core = place_ref[0], place_ref[1]
    chunk = lax.bitwise_and(y - back, 3) * 2 + (1 - core if other else core)
    return (2 * y + core - chunk) * ROWS


STEPS = MINE // TILE
ONES = 8


def part_of(a):
    return TILE * (a + 1), slice(TILE * a, TILE * (a + 1))


def masked(scores, gap, limit, axis=0):
    free = scores.shape[axis] - TILE
    last = lax.slice_in_dim(scores, free, free + TILE, axis=axis)
    last = jnp.where(gap <= limit, last, NEGATIVE)
    if not free:
        return last
    return jnp.concatenate([lax.slice_in_dim(scores, 0, free, axis=axis), last], axis=axis)


def pack(rows):
    halves = rows.reshape(LOCAL, 2, HD, HD)
    return jnp.concatenate([halves[:, 0], halves[:, 1]], axis=2)


def prepare_kernel(mine_ref, pair_ref, columns_ref):
    queries = [unfold(mine_ref[a, ROWS:]).astype(F32) for a in range(LOCAL)]
    queries = jnp.concatenate(queries, axis=0) * (HD**-0.5)
    wide = jnp.concatenate([queries, jnp.zeros((MINE, HD), F32)], axis=1)
    columns_ref[...] = jnp.transpose(wide).astype(BF16)
    for a in range(LOCAL):
        pair_ref[a * ROWS : (a + 1) * ROWS] = mine_ref[a, :ROWS]


def prepare(mine):
    shapes = [((MINE, 2 * HD), BF16), ((2 * HD, MINE), BF16)]
    return local(prepare_kernel, "prepare", shapes, place=False)(mine)


STATS = 48


def three_parts(row):
    block = jnp.concatenate([row[:, i * ROWS : (i + 1) * ROWS] for i in range(LOCAL)], axis=0)
    high = block.astype(BF16).astype(F32)
    middle = (block - high).astype(BF16).astype(F32)
    return jnp.concatenate([high, middle, block - high - middle], axis=0)


def whole_row(parts):
    block = parts[:LOCAL] + parts[LOCAL : 2 * LOCAL] + parts[2 * LOCAL :]
    return jnp.concatenate([block[i : i + 1] for i in range(LOCAL)], axis=1)


def prepare_back_kernel(mixed_ref, turned_ref, q_columns, stat_ref, both_ref, columns_ref, delta_ref):
    grads = [unfold(mixed_ref[a, HD:]).astype(F32) for a in range(LOCAL)]
    grads = jnp.concatenate(grads, axis=0)
    queries = jnp.transpose(q_columns[...].astype(F32))
    columns = jnp.transpose(jnp.concatenate([jnp.zeros((MINE, HD), F32), grads], axis=1))
    columns_ref[...] = columns.astype(BF16)
    both = columns[HD:] * turned_ref[...].astype(F32)
    delta = jnp.sum(both, axis=0, keepdims=True)
    delta_ref[...] = jnp.broadcast_to(delta, (8, MINE))
    both_ref[:MINE] = jnp.concatenate([queries[:, :HD], grads], axis=1).astype(BF16)
    stats = jnp.concatenate([three_parts(stat_ref[0:1]), three_parts(delta)], axis=0)
    both_ref[MINE:] = stats.astype(BF16)


def prepare_back(*args):
    shapes = [((MINE + STATS, 2 * HD), BF16), ((2 * HD, MINE), BF16), ((8, MINE), F32)]
    return local(prepare_back_kernel, "prepare_back", shapes, place=False)(*args)


def forward_kernel(which, first, last, place_ref, columns_ref, *refs):
    chunks, refs = refs[:2], refs[2:]
    if not first:
        (old_total, old_top), refs = refs[:2], refs[2:]
    if last:
        grad_ref, out_ref, turned_ref, stat_ref, total, top = refs
    else:
        total, top = refs
    if first:
        total[...] = jnp.zeros_like(total)
        top[...] = jnp.full_like(top, NEGATIVE)
    else:
        total[...] = old_total[...]
        top[...] = old_top[...]
    gap = frame_gap()
    limits = [chunk_limit(place_ref, back, other) for back, other in which]
    ones = jnp.ones((ONES, MINE), F32)
    values = [
        jnp.concatenate([ones, flip(ref[...])[HD:]], axis=0).astype(BF16) for ref in chunks
    ]

    def scores_of(a):
        count, at = part_of(a)
        return [
            masked(mm(ref[:count], columns_ref[:, at]), gap, limit)
            for ref, limit in zip(chunks, limits, strict=True)
        ]

    scores = scores_of(0)
    for a in range(STEPS):
        now, scores = scores, scores_of(a + 1) if a + 1 < STEPS else None
        count, at = part_of(a)
        old = top[0:1, at]
        new = old
        for score in now:
            new = jnp.maximum(new, jnp.max(score, axis=0, keepdims=True))
        added = total[:, at] * jnp.exp(old - new)
        for score, value in zip(now, values, strict=True):
            added += mm(value[:, :count], jnp.exp(score - new).astype(BF16))
        total[:, at] = added
        top[0:1, at] = new
    if last:
        row_total = total[0:1]
        attended = (total[ONES:] / row_total).astype(BF16).astype(F32)
        stat_ref[...] = jnp.broadcast_to(top[0:1] + jnp.log(row_total), (8, MINE))
        turned_ref[...] = attended.astype(BF16)
        out_ref[:, :HD] = pack(jnp.transpose(attended)).astype(BF16)
        out_ref[:, HD:] = grad_ref[...]


def attend(step, place, columns, group, state=(), grads=None):
    held = [((ONES + HD, MINE), F32), ((8, MINE), F32)]
    last = grads is not None
    outs = [((LOCAL, ROWS, 2 * HD), BF16), ((HD, MINE), BF16), ((8, MINE), F32)]
    kernel = functools.partial(forward_kernel, [c[:2] for c in group], not state, last)
    return local(
        kernel,
        f"attend{step}",
        outs if last else held,
        scratch=[pltpu.VMEM(*h) for h in held] if last else [],
        flops=COST["attend"],
    )(place, columns, *[c[2] for c in group], *state, *([grads] if last else []))


def query_visits(which, place_ref, held, chunks, total):
    q_columns, g_columns, stat_ref, delta_ref = held
    gap = frame_gap()
    limits = [chunk_limit(place_ref, back, other) for back, other in which]
    steps = [(i, a) for i in range(len(which)) for a in range(STEPS)]

    def products(i, a):
        count, at = part_of(a)
        pair = chunks[i][:count]
        return mm(pair, q_columns[:, at]), mm(pair, g_columns[:, at])

    ahead = products(*steps[0])
    for n, (i, a) in enumerate(steps):
        scores, grads = ahead
        if n + 1 < len(steps):
            ahead = products(*steps[n + 1])
        if a == 0:
            turned = flip(chunks[i][...])[:HD].astype(BF16)
        count, at = part_of(a)
        chances = jnp.exp(masked(scores, gap, limits[i]) - stat_ref[0:1, at])
        score_grad = (chances * (grads - delta_ref[0:1, at])).astype(BF16)
        total[:, at] += mm(turned[:, :count], score_grad)


def pair_visits(which, place_ref, own_ref, chunks, total):
    gap = frame_gap()
    keys_side = lax.broadcasted_iota(jnp.int32, (MINE, 2 * HD), 1) < HD
    own = own_ref[...].astype(F32)
    keys = jnp.where(keys_side, own, 0.0).astype(BF16)
    values = jnp.where(keys_side, 0.0, own).astype(BF16)
    limits = [-chunk_limit(place_ref, back, other) for back, other in which]
    steps = [(i, a) for i in range(len(which)) for a in range(STEPS)]
    turned = {}

    def products(i, a):
        if a == 0:
            turned[i] = flip(chunks[i][:MINE]).astype(BF16)
        count, at = part_of(a)
        return mm(keys[:count], turned[i][:, at]), mm(values[:count], turned[i][:, at])

    ahead = products(*steps[0])
    for n, (i, a) in enumerate(steps):
        scores, grads = ahead
        if n + 1 < len(steps):
            ahead = products(*steps[n + 1])
        if a == 0:
            stats = chunks[i][MINE:].astype(F32)
            log_total, delta = whole_row(stats[: STATS // 2]), whole_row(stats[STATS // 2 :])
        count, at = part_of(a)
        chances = jnp.exp(masked(scores, gap, limits[i]) - log_total[:, at])
        score_grad = (chances * (grads - delta[:, at])).astype(BF16)
        key_grads = mm(score_grad, chunks[i][at])
        value_grads = mm(chances.astype(BF16), chunks[i][at])
        total[:count] += jnp.where(keys_side[:count], key_grads, value_grads)


QUERY_TOTAL = ((HD, MINE), F32)
PAIR_TOTAL = ((MINE, 2 * HD), F32)


def query_kernel(which, place_ref, *refs):
    held, (*chunks, total) = refs[:4], refs[4:]
    total[...] = jnp.zeros_like(total)
    query_visits(which, place_ref, held, chunks, total)


def query_pass(place, held, group):
    kernel = functools.partial(query_kernel, [c[:2] for c in group])
    call = local(kernel, "query_pass", [QUERY_TOTAL], flops=COST["attend"])
    return call(place, *held, *[c[2] for c in group])[0]


def both_kernel(which, pair_which, place_ref, *refs):
    held, refs = refs[:4], refs[4:]
    chunks, refs = refs[: len(which)], refs[len(which) :]
    query_chunks, refs = refs[: len(pair_which)], refs[len(pair_which) :]
    own_ref, old_total, out_ref, pair_total, total = refs
    total[...] = old_total[...]
    query_visits(which, place_ref, held, chunks, total)
    out_ref[...] = pack(jnp.transpose(total[...] * (HD**-0.5))).astype(BF16)
    pair_total[...] = jnp.zeros_like(pair_total)
    pair_visits(pair_which, place_ref, own_ref, query_chunks, pair_total)


def both_pass(place, held, group, pair_group, own, state):
    kernel = functools.partial(both_kernel, [c[:2] for c in group], [c[:2] for c in pair_group])
    call = local(
        kernel, "both_pass", [((LOCAL, HD, 2 * HD), BF16), PAIR_TOTAL],
        scratch=[pltpu.VMEM(*QUERY_TOTAL)], flops=2 * COST["attend"],
    )
    return call(place, *held, *[c[2] for c in group + pair_group], own, state)


def pair_kernel(which, place_ref, own_ref, *refs):
    *chunks, old_total, total = refs
    total[...] = old_total[...]
    pair_visits(which, place_ref, own_ref, chunks, total)


def pair_pass(place, own, group, state):
    kernel = functools.partial(pair_kernel, [c[:2] for c in group])
    call = local(kernel, "pair_pass", [PAIR_TOTAL], flops=COST["attend"])
    return call(place, own, *[c[2] for c in group], state)[0]


def last_kernel(which, place_ref, own_ref, *refs):
    chunks, (old_total, query_ref, w0, w1, w3, out_ref, total) = refs[: len(which)], refs[len(which) :]
    total[...] = old_total[...]
    pair_visits(which, place_ref, own_ref, chunks, total)
    out_ref[:, :ROWS] = total[...].astype(BF16).reshape(LOCAL, ROWS, 2 * HD)
    out_ref[:, ROWS:BACK] = query_ref[...]
    parts = sum(ref[...].astype(F32) for ref in (w0, w1, w3)).astype(BF16)
    for i in range(4):
        at = BACK + COLUMNS * i
        out_ref[:, at : at + COLUMNS] = parts[:, :, ROWS * i : ROWS * (i + 1)]


def last_pass(place, own, group, *more):
    kernel = functools.partial(last_kernel, [c[:2] for c in group])
    call = local(
        kernel, "last_pass", [((LOCAL, BACK + ROWS, 2 * HD), BF16)],
        scratch=[pltpu.VMEM(*PAIR_TOTAL)], flops=COST["attend"],
    )
    return call(place, own, *[c[2] for c in group], *more)[0]


def output_kernel(
    place_ref, mixed_ref, g0, g1, g2, g3, weight_ref, kept_ref, sent_ref, *share_refs
):
    core, tp = place_ref[1], place_ref[2]
    attention = jnp.concatenate([unfold(mixed_ref[h, :HD]) for h in range(LOCAL)], axis=1)
    for back, ref in enumerate((g0, g1, g2, g3)):
        at = pl.ds(lax.bitwise_and(tp - back, 3) * 2, 2)
        part = mm(ref[...], attention, 0, 0).reshape(2, 4, 2, COLUMNS, WIDTH)
        for y in range(4):
            ours, theirs = part[:, y, 0], part[:, y, 1]
            kept_ref[y, at] = jnp.where(core == 0, ours, theirs).astype(BF16)
            sent_ref[y, at] = jnp.where(core == 0, theirs, ours).astype(BF16)
    for ahead, ref in enumerate(share_refs):
        ref[...] = mm(attention, weight_ref[:, block_of(place_ref, ahead)]).astype(BF16)


def output_side(place, mixed, grads, weight):
    half, share = ((4, LOCAL, COLUMNS, WIDTH), BF16), ((ROWS, WIDTH), BF16)
    call = local(output_kernel, "output_side", [half] * 2 + [share] * TP, flops=COST["small"])
    kept, sent, *shares = call(place, mixed, *grads, weight)
    return kept, sent, shares


def core_sum_kernel(place_ref, kept_ref, got_ref, *out_refs):
    for ahead, ref in enumerate(out_refs):
        y = lax.bitwise_and(place_ref[0] + ahead, 3)
        ref[...] = (kept_ref[y].astype(F32) + got_ref[y].astype(F32)).astype(BF16)


def core_sum(place, kept, got):
    shapes = [((LOCAL, COLUMNS, WIDTH), BF16)] * 4
    return local(core_sum_kernel, "core_sum", shapes)(place, kept, got)


def add_kernel(left_ref, right_ref, out_ref):
    out_ref[...] = (left_ref[...].astype(F32) + right_ref[...].astype(F32)).astype(BF16)


def add(left, right):
    return local(add_kernel, "add", [(left.shape, BF16)], place=False)(left, right)[0]


def weight_sum_kernel(back_ref, out_ref):
    for i in range(4):
        at = slice(BACK + COLUMNS * i, BACK + COLUMNS * (i + 1))
        out_ref[:, ROWS * i : ROWS * (i + 1)] = sum(
            back_ref[a, at].astype(F32) for a in range(LOCAL)
        )


def weight_sum(back):
    shapes = [((COLUMNS, WIDTH), F32)]
    return local(weight_sum_kernel, "weight_sum", shapes, place=False)(back)[0]


EXTRA = 16


CUT = 80


def split_line(line):
    high = line.astype(BF16).astype(F32)
    middle = (line - high).astype(BF16).astype(F32)
    rows = [high, middle, line - high - middle, jnp.zeros((EXTRA - 3, line.shape[1]), F32)]
    return jnp.concatenate(rows, axis=0)


def triple_kernel(
    place_ref, back_ref, done_ref, share_ref, weight_ref, triple_ref, line_ref, up_ref, down_ref
):
    pairs = [back_ref[h, :ROWS] for h in range(LOCAL)]
    sides = [
        [unfold(back_ref[h, ROWS:BACK]) for h in range(LOCAL)],
        [pair[:, :HD] for pair in pairs],
        [pair[:, HD:] for pair in pairs],
    ]
    centre = jnp.zeros((ROWS, 1), F32)
    for j in range(3):
        side = jnp.concatenate(sides[j], axis=1)
        triple_ref[j] = side
        both = side.astype(F32) * done_ref[j].astype(F32)
        centre += jnp.sum(both, axis=1, keepdims=True)
    line = jnp.transpose(jnp.broadcast_to(centre, (ROWS, ROWS)))[0:1]
    line = jnp.concatenate([line, jnp.zeros((1, WIDTH - ROWS), F32)], axis=1)
    block = split_line(line).astype(BF16)
    line_ref[...] = block
    far = input_part(place_ref, triple_ref, weight_ref, 2).astype(BF16)
    up_ref[:CUT] = far[:CUT]
    up_ref[CUT:] = share_ref[:HALF]
    down_ref[: ROWS - CUT] = far[CUT:]
    down_ref[ROWS - CUT : REST] = block
    down_ref[REST:] = share_ref[HALF:]


HALF = ROWS // 2
REST = ROWS + EXTRA - CUT


def input_part(place_ref, triple_ref, weight_ref, ahead):
    at = block_of(place_ref, ahead)
    return sum(mm(triple_ref[j], weight_ref[j, at], 1, 1) for j in range(3))


def triple_side(place, back, done, share, weight):
    shapes = [
        ((3, ROWS, WIDTH), BF16),
        ((EXTRA, WIDTH), BF16),
        ((CUT + HALF, WIDTH), BF16),
        ((REST + HALF, WIDTH), BF16),
    ]
    call = local(triple_kernel, "triple_side", shapes, flops=COST["small"])
    return call(place, back, done, share, weight)


def input_kernel(place_ref, triple_ref, weight_ref, near_ref, behind_ref, rest_ref):
    for ahead, ref in ((1, near_ref), (3, behind_ref), (0, rest_ref)):
        ref[...] = input_part(place_ref, triple_ref, weight_ref, ahead)


def input_side(place, triple, weight):
    shapes = [((ROWS, WIDTH), F32)] * 3
    return local(input_kernel, "input_side", shapes, flops=COST["small"])(place, triple, weight)


def merge_kernel(
    near_ref, behind_ref, line_ref, share_near, share_behind, up_ref, down_ref, near_out, behind_out
):
    near_out[:CUT] = (near_ref[:CUT] + up_ref[:CUT].astype(F32)).astype(BF16)
    near_out[CUT:ROWS] = near_ref[CUT:].astype(BF16)
    near_out[ROWS : ROWS + EXTRA] = line_ref[...]
    behind_out[:CUT] = behind_ref[:CUT].astype(BF16)
    behind_out[CUT:ROWS] = (
        behind_ref[CUT:] + down_ref[: ROWS - CUT].astype(F32)
    ).astype(BF16)
    lines = line_ref[...].astype(F32) + down_ref[ROWS - CUT : REST].astype(F32)
    behind_out[ROWS : ROWS + EXTRA] = split_line(
        jnp.sum(lines, axis=0, keepdims=True)
    ).astype(BF16)
    at = ROWS + EXTRA
    near_out[at : at + HALF] = (
        share_near[:HALF].astype(F32) + up_ref[CUT:].astype(F32)
    ).astype(BF16)
    near_out[at + HALF :] = share_near[HALF:]
    behind_out[at : at + HALF] = share_behind[:HALF]
    behind_out[at + HALF :] = (
        share_behind[HALF:].astype(F32) + down_ref[REST:].astype(F32)
    ).astype(BF16)


def merge(*args):
    shapes = [((2 * ROWS + EXTRA, WIDTH), BF16)] * 2
    return local(merge_kernel, "merge", shapes, place=False)(*args)


def finish_kernel(
    rest_ref, line_ref, share_ref, p1, p3, summed_ref, inv_ref, grad_ref, layer_ref, out_ref
):
    total = rest_ref[...] + p1[:ROWS].astype(F32) + p3[:ROWS].astype(F32)
    lines = line_ref[...].astype(F32)
    lines += p1[ROWS : ROWS + EXTRA].astype(F32) + p3[ROWS : ROWS + EXTRA].astype(F32)
    line = jnp.sum(lines[:, :ROWS], axis=0, keepdims=True) / (TP * WIDTH)
    centre = jnp.transpose(jnp.broadcast_to(line, (ROWS, ROWS)))[:, 0:1]
    inv = inv_ref[:, 0:1]
    summed = summed_ref[...].astype(F32)
    out_ref[...] = grad_ref[...].astype(F32) + inv * (total - summed * inv * centre)
    shares = (share_ref[...], p1[ROWS + EXTRA :], p3[ROWS + EXTRA :])
    layer_ref[...] = (summed + sum(share.astype(F32) for share in shares)).astype(BF16)


def finish(*args):
    shapes = [((ROWS, WIDTH), BF16), ((ROWS, WIDTH), F32)]
    return local(finish_kernel, "finish", shapes, place=False)(*args)


def ids_before(code_ids):
    route = [(i, i + 1) for i in range(lax.axis_size(SEQ) - 1)]
    return lax.ppermute(code_ids, SEQ, route)


def over_cores(block):
    return lax.ppermute(block, "core", [(0, 1), (1, 0)])


def body(code_ids, delays, embed_table, project_in, project_out, grad_output):
    place = [lax.axis_index(axis) for axis in ("y", "core", "tp")]
    place = jnp.stack(place + [lax.axis_index(SEQ) * ROWS]).astype(jnp.int32)
    place = jnp.concatenate([place, delays])
    weight_in = project_in.transpose(1, 0, 2)
    up_tp, down_tp = [lambda x, k=k: lax.ppermute(x, "tp", ring(k, TP)) for k in (1, -1)]
    up_y, down_y = [lambda x, k=k: lax.ppermute(x, "y", ring(k, 4)) for k in (1, -1)]
    together = lambda *values: lax.optimization_barrier(values)

    summed = embed(place, ids_before(code_ids), code_ids, embed_table)
    s1, s3 = up_tp(summed), down_tp(summed)
    summeds = [summed, s1, up_tp(s1), s3]
    grad, _ = together(grad_output, summed)
    g1, g3 = up_tp(grad), down_tp(grad)
    blocks, done, inv = project(place, summeds, weight_in)
    blocks, g1, g3 = together(blocks, g1, g3)
    mine = lax.all_to_all(blocks, HEADS_OVER, 0, 0, tiled=True)

    own, q_columns = prepare(mine)
    g2 = down_tp(g3)
    y1, y3, mate = up_y(own), down_y(own), over_cores(own)
    state = attend(0, place, q_columns, [(0, 0, own), (0, 1, mate)])
    y1, y3, g2, *state = together(y1, y3, g2, *state)
    other1, other3, y2 = over_cores(y1), over_cores(y3), up_y(y1)
    state = attend(1, place, q_columns, [(1, 0, y1), (3, 0, y3)], state)
    y2, *state = together(y2, *state)
    other2 = over_cores(y2)
    state = attend(2, place, q_columns, [(1, 1, other1), (3, 1, other3)], state)
    grads = [grad, g1, g2, g3]
    grad_heads = grad_side(place, grads, project_out)
    mixed, turned, stat = attend(
        3, place, q_columns, [(2, 0, y2), (2, 1, other2)], state, grad_heads
    )
    mixed = lax.all_to_all(mixed, HEADS_OVER, 0, 0, tiled=True)

    both, g_columns, delta = prepare_back(mixed, turned, q_columns, stat)
    held = (q_columns, g_columns, stat, delta)
    kept, sent, shares = output_side(place, mixed, grads, project_out)
    b1, b3, b_mate, got = up_y(both), down_y(both), over_cores(both), over_cores(sent)
    state = query_pass(
        place, held, [(0, 0, own), (0, 1, mate), (1, 0, y1), (1, 1, other1), (3, 0, y3)]
    )
    b1, b3, b_mate, got, state = together(b1, b3, b_mate, got, state)
    w0, w1, w2, w3 = core_sum(place, kept, got)
    w2, w3, b2 = up_y(w2), down_y(w3), up_y(b1)
    b_other1, b_other3 = over_cores(b1), over_cores(b3)
    query_grads, state = both_pass(
        place,
        held,
        [(2, 0, y2), (2, 1, other2), (3, 1, other3)],
        [(0, 0, both), (0, 1, b_mate), (1, 0, b1)],
        own,
        state,
    )
    w2, w3, b2, b_other1, b_other3, state = together(w2, w3, b2, b_other1, b_other3, state)
    w1, b_other2 = up_y(add(w1, w2)), over_cores(b2)
    state = pair_pass(
        place, own, [(3, 0, b3), (1, 1, b_other1), (3, 1, b_other3)], state
    )
    w1, b_other2, state = together(w1, b_other2, state)
    packed = last_pass(
        place, own, [(2, 0, b2), (2, 1, b_other2)], state, query_grads, w0, w1, w3
    )
    back = lax.all_to_all(packed, HEADS_OVER, 0, 0, tiled=True)

    triple, line, up, down = triple_side(place, back, done, shares[2], weight_in)
    up, down = up_tp(up), down_tp(down)
    near, behind, rest = input_side(place, triple, weight_in)
    near, behind = merge(near, behind, line, shares[1], shares[3], up, down)
    near, behind = up_tp(near), down_tp(behind)
    grad_project_out = weight_sum(back).transpose(1, 0)
    layer_output, grad_embed = finish(
        rest, line, shares[0], near, behind, summed, inv, grad_output
    )
    return layer_output, grad_embed, grad_project_out


def solution(mesh):
    fine = Mesh(mesh.devices.reshape(SPLIT), AXES)
    return jax.shard_map(
        body,
        mesh=fine,
        in_specs=(
            P(None, SEQ),
            P(),
            P(None, None, "tp"),
            P(None, None, "tp"),
            P("tp", None),
            P(SEQ, "tp"),
        ),
        out_specs=(P(SEQ, "tp"), P(SEQ, "tp"), P("tp", SEQ)),
        check_vma=False,
    )
```

```python
import functools

import jax
import jax.numpy as jnp
from jax import lax
from jax.experimental import pallas as pl
from jax.experimental.pallas import tpu as pltpu
from jax.sharding import Mesh, PartitionSpec as P

SPLIT = (2, 4, 4, 2, 4)
AXES = ("zl", "x", "y", "core", "tp")
SEQ = ("zl", "x", "y", "core")
HEADS_OVER = ("zl", "x")

HD = 64
BOOKS = 4
DMAX = 3
VOCAB = 1024
ROWS = 128
WIDTH = 512
LOCAL = 8
TP = 4
COLUMNS = 32
BACK = ROWS + HD
MINE = LOCAL * ROWS
TILE = 256
NEGATIVE = -1e30
EPS = 1e-05
F32 = jnp.float32
BF16 = jnp.bfloat16
MIB = 1024 * 1024
COST = {"small": 4e9, "attend": 5e9}


def mm(left, right, left_axis=1, right_axis=0):
    return lax.dot_general(
        left, right, (((left_axis,), (right_axis,)), ((), ())), preferred_element_type=F32
    )


def ring(distance, count):
    return [(i, (i + distance) % count) for i in range(count)]


def vmem(count):
    return [pl.BlockSpec(memory_space=pltpu.VMEM)] * count


SMEM = pl.BlockSpec(memory_space=pltpu.SMEM)


def local(kernel, name, shapes, scratch=(), flops=0, place=True):
    def call(*args):
        outs = [jax.ShapeDtypeStruct(shape, kind) for shape, kind in shapes]
        moved = sum(a.size * a.dtype.itemsize for a in (*args, *outs))
        return pl.pallas_call(
            kernel,
            in_specs=([SMEM] if place else []) + vmem(len(args) - place),
            out_specs=vmem(len(outs)),
            out_shape=outs,
            scratch_shapes=list(scratch),
            compiler_params=pltpu.CompilerParams(vmem_limit_bytes=16 * MIB),
            cost_estimate=pl.CostEstimate(flops=int(flops), transcendentals=0, bytes_accessed=moved),
            name=name,
        )(*args)

    return call


def block_of(place_ref, step):
    return pl.ds(pl.multiple_of(lax.bitwise_and(place_ref[2] + step, 3) * WIDTH, WIDTH), WIDTH)


def fold(rows):
    return jnp.concatenate([rows[:HD], rows[HD:]], axis=1)


def unfold(folded):
    return jnp.concatenate([folded[:, :HD], folded[:, HD:]], axis=0)


def embed_kernel(place_ref, before_ref, ids_ref, table_ref, out_ref):
    before, ids = before_ref[...], ids_ref[...]
    moved = [ids] + [
        jnp.concatenate([before[:, ROWS - d :], ids[:, : ROWS - d]], axis=1)
        for d in range(1, DMAX + 1)
    ]
    frames = place_ref[3] + lax.broadcasted_iota(jnp.int32, (1, ROWS), 1)
    rows = []
    for book in range(BOOKS):
        delay, row = place_ref[4 + book], moved[0][book : book + 1]
        for d in range(1, DMAX + 1):
            row = jnp.where(delay == d, moved[d][book : book + 1], row)
        rows.append(jnp.where(frames >= delay, row, -1).astype(F32))
    columns = jnp.transpose(jnp.concatenate(rows * 2, axis=0)).astype(jnp.int32)
    entries = lax.broadcasted_iota(jnp.int32, (ROWS, VOCAB), 1)
    total = jnp.zeros((ROWS, WIDTH), F32)
    for book in range(BOOKS):
        chosen = jnp.where(entries == columns[:, book : book + 1], 1.0, 0.0).astype(BF16)
        total += mm(chosen, table_ref[book])
    out_ref[...] = total.astype(BF16)


def embed(place, before, ids, table):
    return local(embed_kernel, "embed", [((ROWS, WIDTH), BF16)])(place, before, ids, table)[0]


def grad_side_kernel(place_ref, g0, g1, g2, g3, weight_ref, out_ref):
    total = jnp.zeros((ROWS, WIDTH), F32)
    for back, ref in enumerate((g0, g1, g2, g3)):
        total += mm(ref[...], weight_ref[:, block_of(place_ref, -back)], 1, 1)
    for h in range(LOCAL):
        out_ref[h] = fold(total[:, h * HD : (h + 1) * HD]).astype(BF16)


def grad_side(place, grads, weight):
    call = local(grad_side_kernel, "grad_side", [((LOCAL, HD, 2 * HD), BF16)], flops=COST["small"])
    return call(place, *grads, weight)[0]


def project_start_kernel(place_ref, s0, s1, s3, weight_ref, total_ref, squares_ref, rest_ref):
    squares = jnp.zeros((ROWS, 1), F32)
    totals = [jnp.zeros((ROWS, WIDTH), F32)] * 3
    for back, ref in ((0, s0), (1, s1), (3, s3)):
        part = ref[...].astype(F32)
        squares += jnp.sum(part * part, axis=1, keepdims=True)
        for j in range(3):
            totals[j] += mm(ref[...], weight_ref[j, block_of(place_ref, -back)])
    for j in range(3):
        total_ref[j] = totals[j]
        rest_ref[j] = weight_ref[j, block_of(place_ref, -2)]
    squares_ref[...] = jnp.broadcast_to(squares, (ROWS, 128))


def project_kernel(s2, rest_ref, total_ref, squares_ref, out_ref, done_ref, inv_ref):
    part = s2[...].astype(F32)
    squares = squares_ref[:, 0:1] + jnp.sum(part * part, axis=1, keepdims=True)
    inv = lax.rsqrt(squares / (TP * WIDTH) + EPS)
    inv_ref[...] = jnp.broadcast_to(inv, (ROWS, 128))
    done = []
    for j in range(3):
        done.append(((total_ref[j] + mm(s2[...], rest_ref[j])) * inv).astype(BF16))
        done_ref[j] = done[j]
    for h in range(LOCAL):
        q, k, v = [part[:, h * HD : (h + 1) * HD] for part in done]
        out_ref[h, :ROWS] = jnp.concatenate([k, v], axis=1)
        out_ref[h, ROWS:] = fold(q)


def project(place, summeds, weight):
    s0, s1, s2, s3 = summeds
    shapes = [((3, ROWS, WIDTH), F32), ((ROWS, 128), F32), ((3, WIDTH, WIDTH), BF16)]
    call = local(project_start_kernel, "project_start", shapes, flops=COST["small"])
    total, squares, rest = call(place, s0, s1, s3, weight)
    shapes = [
        ((LOCAL, BACK, 2 * HD), BF16),
        ((3, ROWS, WIDTH), BF16),
        ((ROWS, 128), F32),
    ]
    call = local(project_kernel, "project", shapes, flops=COST["small"], place=False)
    return call(s2, rest, total, squares)


def flip(block):
    return jnp.transpose(block.astype(F32))


def frame_gap():
    keys = lax.broadcasted_iota(jnp.int32, (TILE, TILE), 0)
    queries = lax.broadcasted_iota(jnp.int32, (TILE, TILE), 1)
    frame = lambda i: lax.shift_right_logical(i, 7) * (LOCAL * ROWS) + lax.bitwise_and(i, ROWS - 1)
    return frame(keys) - frame(queries)


def chunk_limit(place_ref, back, other):
    y, core = place_ref[0], place_ref[1]
    chunk = lax.bitwise_and(y - back, 3) * 2 + (1 - core if other else core)
    return (2 * y + core - chunk) * ROWS


STEPS = MINE // TILE
ONES = 8


def part_of(a):
    return TILE * (a + 1), slice(TILE * a, TILE * (a + 1))


def masked(scores, gap, limit, axis=0):
    free = scores.shape[axis] - TILE
    last = lax.slice_in_dim(scores, free, free + TILE, axis=axis)
    last = jnp.where(gap <= limit, last, NEGATIVE)
    if not free:
        return last
    return jnp.concatenate([lax.slice_in_dim(scores, 0, free, axis=axis), last], axis=axis)


def pack(rows):
    halves = rows.reshape(LOCAL, 2, HD, HD)
    return jnp.concatenate([halves[:, 0], halves[:, 1]], axis=2)


def prepare_kernel(mine_ref, pair_ref, columns_ref):
    queries = [unfold(mine_ref[a, ROWS:]).astype(F32) for a in range(LOCAL)]
    queries = jnp.concatenate(queries, axis=0) * (HD**-0.5)
    wide = jnp.concatenate([queries, jnp.zeros((MINE, HD), F32)], axis=1)
    columns_ref[...] = jnp.transpose(wide).astype(BF16)
    for a in range(LOCAL):
        pair_ref[a * ROWS : (a + 1) * ROWS] = mine_ref[a, :ROWS]


def prepare(mine):
    shapes = [((MINE, 2 * HD), BF16), ((2 * HD, MINE), BF16)]
    return local(prepare_kernel, "prepare", shapes, place=False)(mine)


STATS = 48


def three_parts(row):
    block = jnp.concatenate([row[:, i * ROWS : (i + 1) * ROWS] for i in range(LOCAL)], axis=0)
    high = block.astype(BF16).astype(F32)
    middle = (block - high).astype(BF16).astype(F32)
    return jnp.concatenate([high, middle, block - high - middle], axis=0)


def whole_column(parts):
    block = jnp.transpose(parts[:LOCAL] + parts[LOCAL : 2 * LOCAL] + parts[2 * LOCAL :])
    return jnp.concatenate([block[:, i : i + 1] for i in range(LOCAL)], axis=0)


def prepare_back_kernel(mixed_ref, turned_ref, q_columns, stat_ref, both_ref, columns_ref, delta_ref):
    grads = [unfold(mixed_ref[a, HD:]).astype(F32) for a in range(LOCAL)]
    grads = jnp.concatenate(grads, axis=0)
    queries = jnp.transpose(q_columns[...].astype(F32))
    columns = jnp.transpose(jnp.concatenate([jnp.zeros((MINE, HD), F32), grads], axis=1))
    columns_ref[...] = columns.astype(BF16)
    both = columns[HD:] * turned_ref[...].astype(F32)
    delta = jnp.sum(both, axis=0, keepdims=True)
    delta_ref[...] = jnp.broadcast_to(delta, (8, MINE))
    both_ref[:MINE] = jnp.concatenate([queries[:, :HD], grads], axis=1).astype(BF16)
    stats = jnp.concatenate([three_parts(stat_ref[0:1]), three_parts(delta)], axis=0)
    both_ref[MINE:] = stats.astype(BF16)


def prepare_back(*args):
    shapes = [((MINE + STATS, 2 * HD), BF16), ((2 * HD, MINE), BF16), ((8, MINE), F32)]
    return local(prepare_back_kernel, "prepare_back", shapes, place=False)(*args)


def forward_kernel(which, first, last, place_ref, columns_ref, *refs):
    chunks, refs = refs[:2], refs[2:]
    if not first:
        (old_total, old_top), refs = refs[:2], refs[2:]
    if last:
        grad_ref, out_ref, turned_ref, stat_ref, total, top = refs
    else:
        total, top = refs
    if first:
        total[...] = jnp.zeros_like(total)
        top[...] = jnp.full_like(top, NEGATIVE)
    else:
        total[...] = old_total[...]
        top[...] = old_top[...]
    gap = frame_gap()
    limits = [chunk_limit(place_ref, back, other) for back, other in which]
    ones = jnp.ones((ONES, MINE), F32)
    values = [
        jnp.concatenate([ones, flip(ref[...])[HD:]], axis=0).astype(BF16) for ref in chunks
    ]

    def scores_of(a):
        count, at = part_of(a)
        return [
            masked(mm(ref[:count], columns_ref[:, at]), gap, limit)
            for ref, limit in zip(chunks, limits, strict=True)
        ]

    scores = scores_of(0)
    for a in range(STEPS):
        now, scores = scores, scores_of(a + 1) if a + 1 < STEPS else None
        count, at = part_of(a)
        old = top[0:1, at]
        new = old
        for score in now:
            new = jnp.maximum(new, jnp.max(score, axis=0, keepdims=True))
        added = total[:, at] * jnp.exp(old - new)
        for score, value in zip(now, values, strict=True):
            added += mm(value[:, :count], jnp.exp(score - new).astype(BF16))
        total[:, at] = added
        top[0:1, at] = new
    if last:
        row_total = total[0:1]
        attended = (total[ONES:] / row_total).astype(BF16).astype(F32)
        stat_ref[...] = jnp.broadcast_to(top[0:1] + jnp.log(row_total), (8, MINE))
        turned_ref[...] = attended.astype(BF16)
        out_ref[:, :HD] = pack(jnp.transpose(attended)).astype(BF16)
        out_ref[:, HD:] = grad_ref[...]


def attend(step, place, columns, group, state=(), grads=None):
    held = [((ONES + HD, MINE), F32), ((8, MINE), F32)]
    last = grads is not None
    outs = [((LOCAL, ROWS, 2 * HD), BF16), ((HD, MINE), BF16), ((8, MINE), F32)]
    kernel = functools.partial(forward_kernel, [c[:2] for c in group], not state, last)
    return local(
        kernel,
        f"attend{step}",
        outs if last else held,
        scratch=[pltpu.VMEM(*h) for h in held] if last else [],
        flops=COST["attend"],
    )(place, columns, *[c[2] for c in group], *state, *([grads] if last else []))


def query_visits(which, place_ref, held, chunks, total):
    q_columns, g_columns, stat_ref, delta_ref = held
    gap = frame_gap()
    limits = [chunk_limit(place_ref, back, other) for back, other in which]
    steps = [(i, a) for i in range(len(which)) for a in range(STEPS)]

    def products(i, a):
        count, at = part_of(a)
        pair = chunks[i][:count]
        return mm(pair, q_columns[:, at]), mm(pair, g_columns[:, at])

    ahead = products(*steps[0])
    for n, (i, a) in enumerate(steps):
        scores, grads = ahead
        if n + 1 < len(steps):
            ahead = products(*steps[n + 1])
        if a == 0:
            turned = flip(chunks[i][...])[:HD].astype(BF16)
        count, at = part_of(a)
        chances = jnp.exp(masked(scores, gap, limits[i]) - stat_ref[0:1, at])
        score_grad = (chances * (grads - delta_ref[0:1, at])).astype(BF16)
        total[:, at] += mm(turned[:, :count], score_grad)


def pair_visits(which, place_ref, own_ref, chunks, total):
    gap = -frame_gap()
    turned_own = flip(own_ref[...])
    keys_side = lax.broadcasted_iota(jnp.int32, (2 * HD, MINE), 0) < HD
    keys = jnp.where(keys_side, turned_own, 0.0).astype(BF16)
    values = jnp.where(keys_side, 0.0, turned_own).astype(BF16)
    limits = [-chunk_limit(place_ref, back, other) for back, other in which]
    steps = [(i, a) for i in range(len(which)) for a in range(STEPS)]

    def products(i, a):
        count, at = part_of(a)
        return mm(chunks[i][at], keys[:, :count]), mm(chunks[i][at], values[:, :count])

    ahead = products(*steps[0])
    for n, (i, a) in enumerate(steps):
        scores, grads = ahead
        if n + 1 < len(steps):
            ahead = products(*steps[n + 1])
        if a == 0:
            turned = flip(chunks[i][:MINE]).astype(BF16)
            stats = chunks[i][MINE:].astype(F32)
            log_total, delta = whole_column(stats[: STATS // 2]), whole_column(stats[STATS // 2 :])
        count, at = part_of(a)
        chances = jnp.exp(masked(scores, gap, limits[i], 1) - log_total[at])
        score_grad = (chances * (grads - delta[at])).astype(BF16)
        total[:HD, :count] += mm(turned[:HD, at], score_grad)
        total[HD:, :count] += mm(turned[HD:, at], chances.astype(BF16))


QUERY_TOTAL = ((HD, MINE), F32)
PAIR_TOTAL = ((2 * HD, MINE), F32)


def query_kernel(which, place_ref, *refs):
    held, (*chunks, total) = refs[:4], refs[4:]
    total[...] = jnp.zeros_like(total)
    query_visits(which, place_ref, held, chunks, total)


def query_pass(place, held, group):
    kernel = functools.partial(query_kernel, [c[:2] for c in group])
    call = local(kernel, "query_pass", [QUERY_TOTAL], flops=COST["attend"])
    return call(place, *held, *[c[2] for c in group])[0]


def both_kernel(which, pair_which, place_ref, *refs):
    held, refs = refs[:4], refs[4:]
    chunks, refs = refs[: len(which)], refs[len(which) :]
    query_chunks, refs = refs[: len(pair_which)], refs[len(pair_which) :]
    own_ref, old_total, out_ref, pair_total, total = refs
    total[...] = old_total[...]
    query_visits(which, place_ref, held, chunks, total)
    out_ref[...] = pack(jnp.transpose(total[...] * (HD**-0.5))).astype(BF16)
    pair_total[...] = jnp.zeros_like(pair_total)
    pair_visits(pair_which, place_ref, own_ref, query_chunks, pair_total)


def both_pass(place, held, group, pair_group, own, state):
    kernel = functools.partial(both_kernel, [c[:2] for c in group], [c[:2] for c in pair_group])
    call = local(
        kernel, "both_pass", [((LOCAL, HD, 2 * HD), BF16), PAIR_TOTAL],
        scratch=[pltpu.VMEM(*QUERY_TOTAL)], flops=2 * COST["attend"],
    )
    return call(place, *held, *[c[2] for c in group + pair_group], own, state)


def pair_kernel(which, place_ref, own_ref, *refs):
    *chunks, old_total, total = refs
    total[...] = old_total[...]
    pair_visits(which, place_ref, own_ref, chunks, total)


def pair_pass(place, own, group, state):
    kernel = functools.partial(pair_kernel, [c[:2] for c in group])
    call = local(kernel, "pair_pass", [PAIR_TOTAL], flops=COST["attend"])
    return call(place, own, *[c[2] for c in group], state)[0]


def last_kernel(which, place_ref, own_ref, *refs):
    chunks, (old_total, query_ref, w0, w1, w3, out_ref, total) = refs[: len(which)], refs[len(which) :]
    total[...] = old_total[...]
    pair_visits(which, place_ref, own_ref, chunks, total)
    out_ref[:, :ROWS] = jnp.transpose(total[...]).astype(BF16).reshape(LOCAL, ROWS, 2 * HD)
    out_ref[:, ROWS:BACK] = query_ref[...]
    parts = sum(ref[...].astype(F32) for ref in (w0, w1, w3)).astype(BF16)
    for i in range(4):
        at = BACK + COLUMNS * i
        out_ref[:, at : at + COLUMNS] = parts[:, :, ROWS * i : ROWS * (i + 1)]


def last_pass(place, own, group, *more):
    kernel = functools.partial(last_kernel, [c[:2] for c in group])
    call = local(
        kernel, "last_pass", [((LOCAL, BACK + ROWS, 2 * HD), BF16)],
        scratch=[pltpu.VMEM(*PAIR_TOTAL)], flops=COST["attend"],
    )
    return call(place, own, *[c[2] for c in group], *more)[0]


def output_kernel(
    place_ref, mixed_ref, g0, g1, g2, g3, weight_ref, kept_ref, sent_ref, *share_refs
):
    core, tp = place_ref[1], place_ref[2]
    attention = jnp.concatenate([unfold(mixed_ref[h, :HD]) for h in range(LOCAL)], axis=1)
    for back, ref in enumerate((g0, g1, g2, g3)):
        at = pl.ds(lax.bitwise_and(tp - back, 3) * 2, 2)
        part = mm(ref[...], attention, 0, 0).reshape(2, 4, 2, COLUMNS, WIDTH)
        for y in range(4):
            ours, theirs = part[:, y, 0], part[:, y, 1]
            kept_ref[y, at] = jnp.where(core == 0, ours, theirs).astype(BF16)
            sent_ref[y, at] = jnp.where(core == 0, theirs, ours).astype(BF16)
    for ahead, ref in enumerate(share_refs):
        ref[...] = mm(attention, weight_ref[:, block_of(place_ref, ahead)]).astype(BF16)


def output_side(place, mixed, grads, weight):
    half, share = ((4, LOCAL, COLUMNS, WIDTH), BF16), ((ROWS, WIDTH), BF16)
    call = local(output_kernel, "output_side", [half] * 2 + [share] * TP, flops=COST["small"])
    kept, sent, *shares = call(place, mixed, *grads, weight)
    return kept, sent, shares


def core_sum_kernel(place_ref, kept_ref, got_ref, *out_refs):
    for ahead, ref in enumerate(out_refs):
        y = lax.bitwise_and(place_ref[0] + ahead, 3)
        ref[...] = (kept_ref[y].astype(F32) + got_ref[y].astype(F32)).astype(BF16)


def core_sum(place, kept, got):
    shapes = [((LOCAL, COLUMNS, WIDTH), BF16)] * 4
    return local(core_sum_kernel, "core_sum", shapes)(place, kept, got)


def add_kernel(left_ref, right_ref, out_ref):
    out_ref[...] = (left_ref[...].astype(F32) + right_ref[...].astype(F32)).astype(BF16)


def add(left, right):
    return local(add_kernel, "add", [(left.shape, BF16)], place=False)(left, right)[0]


def weight_sum_kernel(back_ref, out_ref):
    for i in range(4):
        at = slice(BACK + COLUMNS * i, BACK + COLUMNS * (i + 1))
        out_ref[:, ROWS * i : ROWS * (i + 1)] = sum(
            back_ref[a, at].astype(F32) for a in range(LOCAL)
        )


def weight_sum(back):
    shapes = [((COLUMNS, WIDTH), F32)]
    return local(weight_sum_kernel, "weight_sum", shapes, place=False)(back)[0]


EXTRA = 16


CUT = 80


def split_line(line):
    high = line.astype(BF16).astype(F32)
    middle = (line - high).astype(BF16).astype(F32)
    rows = [high, middle, line - high - middle, jnp.zeros((EXTRA - 3, line.shape[1]), F32)]
    return jnp.concatenate(rows, axis=0)


def triple_kernel(
    place_ref, back_ref, done_ref, share_ref, weight_ref, triple_ref, line_ref, up_ref, down_ref
):
    pairs = [back_ref[h, :ROWS] for h in range(LOCAL)]
    sides = [
        [unfold(back_ref[h, ROWS:BACK]) for h in range(LOCAL)],
        [pair[:, :HD] for pair in pairs],
        [pair[:, HD:] for pair in pairs],
    ]
    centre = jnp.zeros((ROWS, 1), F32)
    for j in range(3):
        side = jnp.concatenate(sides[j], axis=1)
        triple_ref[j] = side
        both = side.astype(F32) * done_ref[j].astype(F32)
        centre += jnp.sum(both, axis=1, keepdims=True)
    line = jnp.transpose(jnp.broadcast_to(centre, (ROWS, ROWS)))[0:1]
    line = jnp.concatenate([line, jnp.zeros((1, WIDTH - ROWS), F32)], axis=1)
    block = split_line(line).astype(BF16)
    line_ref[...] = block
    far = input_part(place_ref, triple_ref, weight_ref, 2).astype(BF16)
    up_ref[:CUT] = far[:CUT]
    up_ref[CUT:] = share_ref[:HALF]
    down_ref[: ROWS - CUT] = far[CUT:]
    down_ref[ROWS - CUT : REST] = block
    down_ref[REST:] = share_ref[HALF:]


HALF = ROWS // 2
REST = ROWS + EXTRA - CUT


def input_part(place_ref, triple_ref, weight_ref, ahead):
    at = block_of(place_ref, ahead)
    return sum(mm(triple_ref[j], weight_ref[j, at], 1, 1) for j in range(3))


def triple_side(place, back, done, share, weight):
    shapes = [
        ((3, ROWS, WIDTH), BF16),
        ((EXTRA, WIDTH), BF16),
        ((CUT + HALF, WIDTH), BF16),
        ((REST + HALF, WIDTH), BF16),
    ]
    call = local(triple_kernel, "triple_side", shapes, flops=COST["small"])
    return call(place, back, done, share, weight)


def input_kernel(place_ref, triple_ref, weight_ref, near_ref, behind_ref, rest_ref):
    for ahead, ref in ((1, near_ref), (3, behind_ref), (0, rest_ref)):
        ref[...] = input_part(place_ref, triple_ref, weight_ref, ahead)


def input_side(place, triple, weight):
    shapes = [((ROWS, WIDTH), F32)] * 3
    return local(input_kernel, "input_side", shapes, flops=COST["small"])(place, triple, weight)


def merge_kernel(
    near_ref, behind_ref, line_ref, share_near, share_behind, up_ref, down_ref, near_out, behind_out
):
    near_out[:CUT] = (near_ref[:CUT] + up_ref[:CUT].astype(F32)).astype(BF16)
    near_out[CUT:ROWS] = near_ref[CUT:].astype(BF16)
    near_out[ROWS : ROWS + EXTRA] = line_ref[...]
    behind_out[:CUT] = behind_ref[:CUT].astype(BF16)
    behind_out[CUT:ROWS] = (
        behind_ref[CUT:] + down_ref[: ROWS - CUT].astype(F32)
    ).astype(BF16)
    lines = line_ref[...].astype(F32) + down_ref[ROWS - CUT : REST].astype(F32)
    behind_out[ROWS : ROWS + EXTRA] = split_line(
        jnp.sum(lines, axis=0, keepdims=True)
    ).astype(BF16)
    at = ROWS + EXTRA
    near_out[at : at + HALF] = (
        share_near[:HALF].astype(F32) + up_ref[CUT:].astype(F32)
    ).astype(BF16)
    near_out[at + HALF :] = share_near[HALF:]
    behind_out[at : at + HALF] = share_behind[:HALF]
    behind_out[at + HALF :] = (
        share_behind[HALF:].astype(F32) + down_ref[REST:].astype(F32)
    ).astype(BF16)


def merge(*args):
    shapes = [((2 * ROWS + EXTRA, WIDTH), BF16)] * 2
    return local(merge_kernel, "merge", shapes, place=False)(*args)


def finish_kernel(
    rest_ref, line_ref, share_ref, p1, p3, summed_ref, inv_ref, grad_ref, layer_ref, out_ref
):
    total = rest_ref[...] + p1[:ROWS].astype(F32) + p3[:ROWS].astype(F32)
    lines = line_ref[...].astype(F32)
    lines += p1[ROWS : ROWS + EXTRA].astype(F32) + p3[ROWS : ROWS + EXTRA].astype(F32)
    line = jnp.sum(lines[:, :ROWS], axis=0, keepdims=True) / (TP * WIDTH)
    centre = jnp.transpose(jnp.broadcast_to(line, (ROWS, ROWS)))[:, 0:1]
    inv = inv_ref[:, 0:1]
    summed = summed_ref[...].astype(F32)
    out_ref[...] = grad_ref[...].astype(F32) + inv * (total - summed * inv * centre)
    shares = (share_ref[...], p1[ROWS + EXTRA :], p3[ROWS + EXTRA :])
    layer_ref[...] = (summed + sum(share.astype(F32) for share in shares)).astype(BF16)


def finish(*args):
    shapes = [((ROWS, WIDTH), BF16), ((ROWS, WIDTH), F32)]
    return local(finish_kernel, "finish", shapes, place=False)(*args)


def ids_before(code_ids):
    route = [(i, i + 1) for i in range(lax.axis_size(SEQ) - 1)]
    return lax.ppermute(code_ids, SEQ, route)


def over_cores(block):
    return lax.ppermute(block, "core", [(0, 1), (1, 0)])


def body(code_ids, delays, embed_table, project_in, project_out, grad_output):
    place = [lax.axis_index(axis) for axis in ("y", "core", "tp")]
    place = jnp.stack(place + [lax.axis_index(SEQ) * ROWS]).astype(jnp.int32)
    place = jnp.concatenate([place, delays])
    weight_in = project_in.transpose(1, 0, 2)
    up_tp, down_tp = [lambda x, k=k: lax.ppermute(x, "tp", ring(k, TP)) for k in (1, -1)]
    up_y, down_y = [lambda x, k=k: lax.ppermute(x, "y", ring(k, 4)) for k in (1, -1)]
    together = lambda *values: lax.optimization_barrier(values)

    summed = embed(place, ids_before(code_ids), code_ids, embed_table)
    s1, s3 = up_tp(summed), down_tp(summed)
    summeds = [summed, s1, up_tp(s1), s3]
    grad, _ = together(grad_output, summed)
    g1, g3 = up_tp(grad), down_tp(grad)
    blocks, done, inv = project(place, summeds, weight_in)
    blocks, g1, g3 = together(blocks, g1, g3)
    mine = lax.all_to_all(blocks, HEADS_OVER, 0, 0, tiled=True)

    own, q_columns = prepare(mine)
    y1, y3, mate = up_y(own), down_y(own), over_cores(own)
    g2 = down_tp(g3)
    state = attend(0, place, q_columns, [(0, 0, own), (0, 1, mate)])
    y1, y3, g2, *state = together(y1, y3, g2, *state)
    other1, other3, y2 = over_cores(y1), over_cores(y3), up_y(y1)
    state = attend(1, place, q_columns, [(1, 0, y1), (3, 0, y3)], state)
    y2, *state = together(y2, *state)
    other2 = over_cores(y2)
    state = attend(2, place, q_columns, [(1, 1, other1), (3, 1, other3)], state)
    grads = [grad, g1, g2, g3]
    grad_heads = grad_side(place, grads, project_out)
    mixed, turned, stat = attend(
        3, place, q_columns, [(2, 0, y2), (2, 1, other2)], state, grad_heads
    )
    mixed = lax.all_to_all(mixed, HEADS_OVER, 0, 0, tiled=True)

    both, g_columns, delta = prepare_back(mixed, turned, q_columns, stat)
    held = (q_columns, g_columns, stat, delta)
    kept, sent, shares = output_side(place, mixed, grads, project_out)
    b1, b3, b_mate, got = up_y(both), down_y(both), over_cores(both), over_cores(sent)
    state = query_pass(
        place, held, [(0, 0, own), (0, 1, mate), (1, 0, y1), (1, 1, other1), (3, 0, y3)]
    )
    b1, b3, b_mate, got, state = together(b1, b3, b_mate, got, state)
    w0, w1, w2, w3 = core_sum(place, kept, got)
    w2, w3, b2 = up_y(w2), down_y(w3), up_y(b1)
    b_other1, b_other3 = over_cores(b1), over_cores(b3)
    query_grads, state = both_pass(
        place,
        held,
        [(2, 0, y2), (2, 1, other2), (3, 1, other3)],
        [(0, 0, both), (0, 1, b_mate), (1, 0, b1)],
        own,
        state,
    )
    w2, w3, b2, b_other1, b_other3, state = together(w2, w3, b2, b_other1, b_other3, state)
    w1, b_other2 = up_y(add(w1, w2)), over_cores(b2)
    state = pair_pass(
        place, own, [(3, 0, b3), (1, 1, b_other1), (3, 1, b_other3)], state
    )
    w1, b_other2, state = together(w1, b_other2, state)
    packed = last_pass(
        place, own, [(2, 0, b2), (2, 1, b_other2)], state, query_grads, w0, w1, w3
    )
    back = lax.all_to_all(packed, HEADS_OVER, 0, 0, tiled=True)

    triple, line, up, down = triple_side(place, back, done, shares[2], weight_in)
    up, down = up_tp(up), down_tp(down)
    near, behind, rest = input_side(place, triple, weight_in)
    near, behind = merge(near, behind, line, shares[1], shares[3], up, down)
    near, behind = up_tp(near), down_tp(behind)
    grad_project_out = weight_sum(back).transpose(1, 0)
    layer_output, grad_embed = finish(
        rest, line, shares[0], near, behind, summed, inv, grad_output
    )
    return layer_output, grad_embed, grad_project_out


def solution(mesh):
    fine = Mesh(mesh.devices.reshape(SPLIT), AXES)
    return jax.shard_map(
        body,
        mesh=fine,
        in_specs=(
            P(None, SEQ),
            P(),
            P(None, None, "tp"),
            P(None, None, "tp"),
            P("tp", None),
            P(SEQ, "tp"),
        ),
        out_specs=(P(SEQ, "tp"), P(SEQ, "tp"), P("tp", SEQ)),
        check_vma=False,
    )
```

```python
import functools

import jax
import jax.numpy as jnp
from jax import lax
from jax.experimental import pallas as pl
from jax.experimental.pallas import tpu as pltpu
from jax.sharding import Mesh, PartitionSpec as P

SPLIT = (2, 4, 4, 2, 4)
AXES = ("zl", "x", "y", "core", "tp")
SEQ = ("zl", "x", "y", "core")
HEADS_OVER = ("zl", "x")

HD = 64
BOOKS = 4
DMAX = 3
VOCAB = 1024
ROWS = 128
WIDTH = 512
LOCAL = 8
TP = 4
COLUMNS = 32
BACK = ROWS + HD
MINE = LOCAL * ROWS
TILE = 256
NEGATIVE = -1e30
EPS = 1e-05
F32 = jnp.float32
BF16 = jnp.bfloat16
MIB = 1024 * 1024
COST = {"small": 4e9, "attend": 5e9}


def mm(left, right, left_axis=1, right_axis=0):
    return lax.dot_general(
        left, right, (((left_axis,), (right_axis,)), ((), ())), preferred_element_type=F32
    )


def ring(distance, count):
    return [(i, (i + distance) % count) for i in range(count)]


def vmem(count):
    return [pl.BlockSpec(memory_space=pltpu.VMEM)] * count


SMEM = pl.BlockSpec(memory_space=pltpu.SMEM)


def local(kernel, name, shapes, scratch=(), flops=0, place=True):
    def call(*args):
        outs = [jax.ShapeDtypeStruct(shape, kind) for shape, kind in shapes]
        moved = sum(a.size * a.dtype.itemsize for a in (*args, *outs))
        return pl.pallas_call(
            kernel,
            in_specs=([SMEM] if place else []) + vmem(len(args) - place),
            out_specs=vmem(len(outs)),
            out_shape=outs,
            scratch_shapes=list(scratch),
            compiler_params=pltpu.CompilerParams(vmem_limit_bytes=16 * MIB),
            cost_estimate=pl.CostEstimate(flops=int(flops), transcendentals=0, bytes_accessed=moved),
            name=name,
        )(*args)

    return call


def block_of(place_ref, step):
    return pl.ds(pl.multiple_of(lax.bitwise_and(place_ref[2] + step, 3) * WIDTH, WIDTH), WIDTH)


def fold(rows):
    return jnp.concatenate([rows[:HD], rows[HD:]], axis=1)


def unfold(folded):
    return jnp.concatenate([folded[:, :HD], folded[:, HD:]], axis=0)


def embed_kernel(place_ref, before_ref, ids_ref, table_ref, out_ref):
    before, ids = before_ref[...], ids_ref[...]
    moved = [ids] + [
        jnp.concatenate([before[:, ROWS - d :], ids[:, : ROWS - d]], axis=1)
        for d in range(1, DMAX + 1)
    ]
    frames = place_ref[3] + lax.broadcasted_iota(jnp.int32, (1, ROWS), 1)
    rows = []
    for book in range(BOOKS):
        delay, row = place_ref[4 + book], moved[0][book : book + 1]
        for d in range(1, DMAX + 1):
            row = jnp.where(delay == d, moved[d][book : book + 1], row)
        rows.append(jnp.where(frames >= delay, row, -1).astype(F32))
    columns = jnp.transpose(jnp.concatenate(rows * 2, axis=0)).astype(jnp.int32)
    entries = lax.broadcasted_iota(jnp.int32, (ROWS, VOCAB), 1)
    total = jnp.zeros((ROWS, WIDTH), F32)
    for book in range(BOOKS):
        chosen = jnp.where(entries == columns[:, book : book + 1], 1.0, 0.0).astype(BF16)
        total += mm(chosen, table_ref[book])
    out_ref[...] = total.astype(BF16)


def embed(place, before, ids, table):
    return local(embed_kernel, "embed", [((ROWS, WIDTH), BF16)])(place, before, ids, table)[0]


def grad_side_kernel(place_ref, g0, g1, g2, g3, weight_ref, out_ref):
    total = jnp.zeros((ROWS, WIDTH), F32)
    for back, ref in enumerate((g0, g1, g2, g3)):
        total += mm(ref[...], weight_ref[:, block_of(place_ref, -back)], 1, 1)
    for h in range(LOCAL):
        out_ref[h] = fold(total[:, h * HD : (h + 1) * HD]).astype(BF16)


def grad_side(place, grads, weight):
    call = local(grad_side_kernel, "grad_side", [((LOCAL, HD, 2 * HD), BF16)], flops=COST["small"])
    return call(place, *grads, weight)[0]


def project_start_kernel(place_ref, s0, s1, s3, weight_ref, total_ref, squares_ref, rest_ref):
    squares = jnp.zeros((ROWS, 1), F32)
    totals = [jnp.zeros((ROWS, WIDTH), F32)] * 3
    for back, ref in ((0, s0), (1, s1), (3, s3)):
        part = ref[...].astype(F32)
        squares += jnp.sum(part * part, axis=1, keepdims=True)
        for j in range(3):
            totals[j] += mm(ref[...], weight_ref[j, block_of(place_ref, -back)])
    for j in range(3):
        total_ref[j] = totals[j]
        rest_ref[j] = weight_ref[j, block_of(place_ref, -2)]
    squares_ref[...] = jnp.broadcast_to(squares, (ROWS, 128))


def project_kernel(s2, rest_ref, total_ref, squares_ref, out_ref, done_ref, inv_ref):
    part = s2[...].astype(F32)
    squares = squares_ref[:, 0:1] + jnp.sum(part * part, axis=1, keepdims=True)
    inv = lax.rsqrt(squares / (TP * WIDTH) + EPS)
    inv_ref[...] = jnp.broadcast_to(inv, (ROWS, 128))
    done = []
    for j in range(3):
        done.append(((total_ref[j] + mm(s2[...], rest_ref[j])) * inv).astype(BF16))
        done_ref[j] = done[j]
    for h in range(LOCAL):
        q, k, v = [part[:, h * HD : (h + 1) * HD] for part in done]
        out_ref[h, :ROWS] = jnp.concatenate([k, v], axis=1)
        out_ref[h, ROWS:] = fold(q)


def project(place, summeds, weight):
    s0, s1, s2, s3 = summeds
    shapes = [((3, ROWS, WIDTH), F32), ((ROWS, 128), F32), ((3, WIDTH, WIDTH), BF16)]
    call = local(project_start_kernel, "project_start", shapes, flops=COST["small"])
    total, squares, rest = call(place, s0, s1, s3, weight)
    shapes = [
        ((LOCAL, BACK, 2 * HD), BF16),
        ((3, ROWS, WIDTH), BF16),
        ((ROWS, 128), F32),
    ]
    call = local(project_kernel, "project", shapes, flops=COST["small"], place=False)
    return call(s2, rest, total, squares)


def flip(block):
    return jnp.transpose(block.astype(F32))


def frame_gap():
    keys = lax.broadcasted_iota(jnp.int32, (TILE, TILE), 0)
    queries = lax.broadcasted_iota(jnp.int32, (TILE, TILE), 1)
    frame = lambda i: lax.shift_right_logical(i, 7) * (LOCAL * ROWS) + lax.bitwise_and(i, ROWS - 1)
    return frame(keys) - frame(queries)


def chunk_limit(place_ref, back, other):
    y, core = place_ref[0], place_ref[1]
    chunk = lax.bitwise_and(y - back, 3) * 2 + (1 - core if other else core)
    return (2 * y + core - chunk) * ROWS


STEPS = MINE // TILE
ONES = 8


def part_of(a):
    return TILE * (a + 1), slice(TILE * a, TILE * (a + 1))


def masked(scores, gap, limit, axis=0):
    free = scores.shape[axis] - TILE
    last = lax.slice_in_dim(scores, free, free + TILE, axis=axis)
    last = jnp.where(gap <= limit, last, NEGATIVE)
    if not free:
        return last
    return jnp.concatenate([lax.slice_in_dim(scores, 0, free, axis=axis), last], axis=axis)


def pack(rows):
    halves = rows.reshape(LOCAL, 2, HD, HD)
    return jnp.concatenate([halves[:, 0], halves[:, 1]], axis=2)


def prepare_kernel(mine_ref, pair_ref, columns_ref):
    queries = [unfold(mine_ref[a, ROWS:]).astype(F32) for a in range(LOCAL)]
    queries = jnp.concatenate(queries, axis=0) * (HD**-0.5)
    wide = jnp.concatenate([queries, jnp.zeros((MINE, HD), F32)], axis=1)
    columns_ref[...] = jnp.transpose(wide).astype(BF16)
    for a in range(LOCAL):
        pair_ref[a * ROWS : (a + 1) * ROWS] = mine_ref[a, :ROWS]


def prepare(mine):
    shapes = [((MINE, 2 * HD), BF16), ((2 * HD, MINE), BF16)]
    return local(prepare_kernel, "prepare", shapes, place=False)(mine)


STATS = 48


def three_parts(row):
    block = jnp.concatenate([row[:, i * ROWS : (i + 1) * ROWS] for i in range(LOCAL)], axis=0)
    high = block.astype(BF16).astype(F32)
    middle = (block - high).astype(BF16).astype(F32)
    return jnp.concatenate([high, middle, block - high - middle], axis=0)


def whole_column(parts):
    block = jnp.transpose(parts[:LOCAL] + parts[LOCAL : 2 * LOCAL] + parts[2 * LOCAL :])
    return jnp.concatenate([block[:, i : i + 1] for i in range(LOCAL)], axis=0)


def prepare_back_kernel(mixed_ref, turned_ref, q_columns, stat_ref, both_ref, columns_ref, delta_ref):
    grads = [unfold(mixed_ref[a, HD:]).astype(F32) for a in range(LOCAL)]
    grads = jnp.concatenate(grads, axis=0)
    queries = jnp.transpose(q_columns[...].astype(F32))
    columns = jnp.transpose(jnp.concatenate([jnp.zeros((MINE, HD), F32), grads], axis=1))
    columns_ref[...] = columns.astype(BF16)
    both = columns[HD:] * turned_ref[...].astype(F32)
    delta = jnp.sum(both, axis=0, keepdims=True)
    delta_ref[...] = jnp.broadcast_to(delta, (8, MINE))
    both_ref[:MINE] = jnp.concatenate([queries[:, :HD], grads], axis=1).astype(BF16)
    stats = jnp.concatenate([three_parts(stat_ref[0:1]), three_parts(delta)], axis=0)
    both_ref[MINE:] = stats.astype(BF16)


def prepare_back(*args):
    shapes = [((MINE + STATS, 2 * HD), BF16), ((2 * HD, MINE), BF16), ((8, MINE), F32)]
    return local(prepare_back_kernel, "prepare_back", shapes, place=False)(*args)


def forward_kernel(which, first, last, place_ref, columns_ref, *refs):
    chunks, refs = refs[:2], refs[2:]
    if not first:
        (old_total, old_top), refs = refs[:2], refs[2:]
    if last:
        grad_ref, out_ref, turned_ref, stat_ref, total, top = refs
    else:
        total, top = refs
    if first:
        total[...] = jnp.zeros_like(total)
        top[...] = jnp.full_like(top, NEGATIVE)
    else:
        total[...] = old_total[...]
        top[...] = old_top[...]
    gap = frame_gap()
    limits = [chunk_limit(place_ref, back, other) for back, other in which]
    ones = jnp.ones((ONES, MINE), F32)
    values = [
        jnp.concatenate([ones, flip(ref[...])[HD:]], axis=0).astype(BF16) for ref in chunks
    ]

    def scores_of(a):
        count, at = part_of(a)
        return [
            masked(mm(ref[:count], columns_ref[:, at]), gap, limit)
            for ref, limit in zip(chunks, limits, strict=True)
        ]

    scores = scores_of(0)
    for a in range(STEPS):
        now, scores = scores, scores_of(a + 1) if a + 1 < STEPS else None
        count, at = part_of(a)
        old = top[0:1, at]
        new = old
        for score in now:
            new = jnp.maximum(new, jnp.max(score, axis=0, keepdims=True))
        added = total[:, at] * jnp.exp(old - new)
        for score, value in zip(now, values, strict=True):
            added += mm(value[:, :count], jnp.exp(score - new).astype(BF16))
        total[:, at] = added
        top[0:1, at] = new
    if last:
        row_total = total[0:1]
        attended = (total[ONES:] / row_total).astype(BF16).astype(F32)
        stat_ref[...] = jnp.broadcast_to(top[0:1] + jnp.log(row_total), (8, MINE))
        turned_ref[...] = attended.astype(BF16)
        out_ref[:, :HD] = pack(jnp.transpose(attended)).astype(BF16)
        out_ref[:, HD:] = grad_ref[...]


def attend(step, place, columns, group, state=(), grads=None):
    held = [((ONES + HD, MINE), F32), ((8, MINE), F32)]
    last = grads is not None
    outs = [((LOCAL, ROWS, 2 * HD), BF16), ((HD, MINE), BF16), ((8, MINE), F32)]
    kernel = functools.partial(forward_kernel, [c[:2] for c in group], not state, last)
    return local(
        kernel,
        f"attend{step}",
        outs if last else held,
        scratch=[pltpu.VMEM(*h) for h in held] if last else [],
        flops=COST["attend"],
    )(place, columns, *[c[2] for c in group], *state, *([grads] if last else []))


def nth(values, i):
    picked = values[0]
    for n, value in enumerate(values[1:], 1):
        picked = jnp.where(i == n, value, picked)
    return picked


def query_visits(which, place_ref, held, chunks, total, store):
    q_columns, g_columns, stat_ref, delta_ref = held
    gap = frame_gap()
    limits = [chunk_limit(place_ref, back, other) for back, other in which]
    for i, ref in enumerate(chunks):
        store[i] = ref[...]

    def visit(i, carried):
        chunk = store.at[i]
        limit = nth(limits, i)

        def products(a):
            count, at = part_of(a)
            pair = chunk[:count]
            return mm(pair, q_columns[:, at]), mm(pair, g_columns[:, at])

        ahead = products(0)
        turned = flip(chunk[...])[:HD].astype(BF16)
        for a in range(STEPS):
            scores, grads = ahead
            if a + 1 < STEPS:
                ahead = products(a + 1)
            count, at = part_of(a)
            chances = jnp.exp(masked(scores, gap, limit) - stat_ref[0:1, at])
            score_grad = (chances * (grads - delta_ref[0:1, at])).astype(BF16)
            total[:, at] += mm(turned[:, :count], score_grad)
        return carried

    lax.fori_loop(0, len(which), visit, 0)


def pair_visits(which, place_ref, own_ref, chunks, total, store):
    gap = -frame_gap()
    turned_own = flip(own_ref[...])
    keys_side = lax.broadcasted_iota(jnp.int32, (2 * HD, MINE), 0) < HD
    keys = jnp.where(keys_side, turned_own, 0.0).astype(BF16)
    values = jnp.where(keys_side, 0.0, turned_own).astype(BF16)
    limits = [-chunk_limit(place_ref, back, other) for back, other in which]
    for i, ref in enumerate(chunks):
        store[i] = ref[...]

    def visit(i, carried):
        chunk = store.at[i]
        limit = nth(limits, i)

        def products(a):
            count, at = part_of(a)
            return mm(chunk[at], keys[:, :count]), mm(chunk[at], values[:, :count])

        ahead = products(0)
        turned = flip(chunk[:MINE]).astype(BF16)
        stats = chunk[MINE:].astype(F32)
        log_total, delta = whole_column(stats[: STATS // 2]), whole_column(stats[STATS // 2 :])
        for a in range(STEPS):
            scores, grads = ahead
            if a + 1 < STEPS:
                ahead = products(a + 1)
            count, at = part_of(a)
            chances = jnp.exp(masked(scores, gap, limit, 1) - log_total[at])
            score_grad = (chances * (grads - delta[at])).astype(BF16)
            total[:HD, :count] += mm(turned[:HD, at], score_grad)
            total[HD:, :count] += mm(turned[HD:, at], chances.astype(BF16))
        return carried

    lax.fori_loop(0, len(which), visit, 0)


def store_of(group):
    return pltpu.VMEM((len(group), *group[0][2].shape), BF16)


QUERY_TOTAL = ((HD, MINE), F32)
PAIR_TOTAL = ((2 * HD, MINE), F32)


def query_kernel(which, place_ref, *refs):
    held, (*chunks, total, store) = refs[:4], refs[4:]
    total[...] = jnp.zeros_like(total)
    query_visits(which, place_ref, held, chunks, total, store)


def query_pass(place, held, group):
    kernel = functools.partial(query_kernel, [c[:2] for c in group])
    call = local(
        kernel, "query_pass", [QUERY_TOTAL], scratch=[store_of(group)], flops=COST["attend"]
    )
    return call(place, *held, *[c[2] for c in group])[0]


def both_kernel(which, pair_which, place_ref, *refs):
    held, refs = refs[:4], refs[4:]
    chunks, refs = refs[: len(which)], refs[len(which) :]
    query_chunks, refs = refs[: len(pair_which)], refs[len(pair_which) :]
    own_ref, old_total, out_ref, pair_total, total, store, pair_store = refs
    total[...] = old_total[...]
    query_visits(which, place_ref, held, chunks, total, store)
    out_ref[...] = pack(jnp.transpose(total[...] * (HD**-0.5))).astype(BF16)
    pair_total[...] = jnp.zeros_like(pair_total)
    pair_visits(pair_which, place_ref, own_ref, query_chunks, pair_total, pair_store)


def both_pass(place, held, group, pair_group, own, state):
    kernel = functools.partial(both_kernel, [c[:2] for c in group], [c[:2] for c in pair_group])
    call = local(
        kernel, "both_pass", [((LOCAL, HD, 2 * HD), BF16), PAIR_TOTAL],
        scratch=[pltpu.VMEM(*QUERY_TOTAL), store_of(group), store_of(pair_group)],
        flops=2 * COST["attend"],
    )
    return call(place, *held, *[c[2] for c in group + pair_group], own, state)


def pair_kernel(which, place_ref, own_ref, *refs):
    *chunks, old_total, total, store = refs
    total[...] = old_total[...]
    pair_visits(which, place_ref, own_ref, chunks, total, store)


def pair_pass(place, own, group, state):
    kernel = functools.partial(pair_kernel, [c[:2] for c in group])
    call = local(
        kernel, "pair_pass", [PAIR_TOTAL], scratch=[store_of(group)], flops=COST["attend"]
    )
    return call(place, own, *[c[2] for c in group], state)[0]


def last_kernel(which, place_ref, own_ref, *refs):
    chunks, refs = refs[: len(which)], refs[len(which) :]
    old_total, query_ref, w0, w1, w3, out_ref, total, store = refs
    total[...] = old_total[...]
    pair_visits(which, place_ref, own_ref, chunks, total, store)
    out_ref[:, :ROWS] = jnp.transpose(total[...]).astype(BF16).reshape(LOCAL, ROWS, 2 * HD)
    out_ref[:, ROWS:BACK] = query_ref[...]
    parts = sum(ref[...].astype(F32) for ref in (w0, w1, w3)).astype(BF16)
    for i in range(4):
        at = BACK + COLUMNS * i
        out_ref[:, at : at + COLUMNS] = parts[:, :, ROWS * i : ROWS * (i + 1)]


def last_pass(place, own, group, *more):
    kernel = functools.partial(last_kernel, [c[:2] for c in group])
    call = local(
        kernel, "last_pass", [((LOCAL, BACK + ROWS, 2 * HD), BF16)],
        scratch=[pltpu.VMEM(*PAIR_TOTAL), store_of(group)], flops=COST["attend"],
    )
    return call(place, own, *[c[2] for c in group], *more)[0]


def output_kernel(
    place_ref, mixed_ref, g0, g1, g2, g3, weight_ref, kept_ref, sent_ref, *share_refs
):
    core, tp = place_ref[1], place_ref[2]
    attention = jnp.concatenate([unfold(mixed_ref[h, :HD]) for h in range(LOCAL)], axis=1)
    for back, ref in enumerate((g0, g1, g2, g3)):
        at = pl.ds(lax.bitwise_and(tp - back, 3) * 2, 2)
        part = mm(ref[...], attention, 0, 0).reshape(2, 4, 2, COLUMNS, WIDTH)
        for y in range(4):
            ours, theirs = part[:, y, 0], part[:, y, 1]
            kept_ref[y, at] = jnp.where(core == 0, ours, theirs).astype(BF16)
            sent_ref[y, at] = jnp.where(core == 0, theirs, ours).astype(BF16)
    for ahead, ref in enumerate(share_refs):
        ref[...] = mm(attention, weight_ref[:, block_of(place_ref, ahead)]).astype(BF16)


def output_side(place, mixed, grads, weight):
    half, share = ((4, LOCAL, COLUMNS, WIDTH), BF16), ((ROWS, WIDTH), BF16)
    call = local(output_kernel, "output_side", [half] * 2 + [share] * TP, flops=COST["small"])
    kept, sent, *shares = call(place, mixed, *grads, weight)
    return kept, sent, shares


def core_sum_kernel(place_ref, kept_ref, got_ref, *out_refs):
    for ahead, ref in enumerate(out_refs):
        y = lax.bitwise_and(place_ref[0] + ahead, 3)
        ref[...] = (kept_ref[y].astype(F32) + got_ref[y].astype(F32)).astype(BF16)


def core_sum(place, kept, got):
    shapes = [((LOCAL, COLUMNS, WIDTH), BF16)] * 4
    return local(core_sum_kernel, "core_sum", shapes)(place, kept, got)


def add_kernel(left_ref, right_ref, out_ref):
    out_ref[...] = (left_ref[...].astype(F32) + right_ref[...].astype(F32)).astype(BF16)


def add(left, right):
    return local(add_kernel, "add", [(left.shape, BF16)], place=False)(left, right)[0]


def weight_sum_kernel(back_ref, out_ref):
    for i in range(4):
        at = slice(BACK + COLUMNS * i, BACK + COLUMNS * (i + 1))
        out_ref[:, ROWS * i : ROWS * (i + 1)] = sum(
            back_ref[a, at].astype(F32) for a in range(LOCAL)
        )


def weight_sum(back):
    shapes = [((COLUMNS, WIDTH), F32)]
    return local(weight_sum_kernel, "weight_sum", shapes, place=False)(back)[0]


EXTRA = 16


CUT = 80


def split_line(line):
    high = line.astype(BF16).astype(F32)
    middle = (line - high).astype(BF16).astype(F32)
    rows = [high, middle, line - high - middle, jnp.zeros((EXTRA - 3, line.shape[1]), F32)]
    return jnp.concatenate(rows, axis=0)


def triple_kernel(
    place_ref, back_ref, done_ref, share_ref, weight_ref, triple_ref, line_ref, up_ref, down_ref
):
    pairs = [back_ref[h, :ROWS] for h in range(LOCAL)]
    sides = [
        [unfold(back_ref[h, ROWS:BACK]) for h in range(LOCAL)],
        [pair[:, :HD] for pair in pairs],
        [pair[:, HD:] for pair in pairs],
    ]
    centre = jnp.zeros((ROWS, 1), F32)
    for j in range(3):
        side = jnp.concatenate(sides[j], axis=1)
        triple_ref[j] = side
        both = side.astype(F32) * done_ref[j].astype(F32)
        centre += jnp.sum(both, axis=1, keepdims=True)
    line = jnp.transpose(jnp.broadcast_to(centre, (ROWS, ROWS)))[0:1]
    line = jnp.concatenate([line, jnp.zeros((1, WIDTH - ROWS), F32)], axis=1)
    block = split_line(line).astype(BF16)
    line_ref[...] = block
    far = input_part(place_ref, triple_ref, weight_ref, 2).astype(BF16)
    up_ref[:CUT] = far[:CUT]
    up_ref[CUT:] = share_ref[:HALF]
    down_ref[: ROWS - CUT] = far[CUT:]
    down_ref[ROWS - CUT : REST] = block
    down_ref[REST:] = share_ref[HALF:]


HALF = ROWS // 2
REST = ROWS + EXTRA - CUT


def input_part(place_ref, triple_ref, weight_ref, ahead):
    at = block_of(place_ref, ahead)
    return sum(mm(triple_ref[j], weight_ref[j, at], 1, 1) for j in range(3))


def triple_side(place, back, done, share, weight):
    shapes = [
        ((3, ROWS, WIDTH), BF16),
        ((EXTRA, WIDTH), BF16),
        ((CUT + HALF, WIDTH), BF16),
        ((REST + HALF, WIDTH), BF16),
    ]
    call = local(triple_kernel, "triple_side", shapes, flops=COST["small"])
    return call(place, back, done, share, weight)


def input_kernel(place_ref, triple_ref, weight_ref, near_ref, behind_ref, rest_ref):
    for ahead, ref in ((1, near_ref), (3, behind_ref), (0, rest_ref)):
        ref[...] = input_part(place_ref, triple_ref, weight_ref, ahead)


def input_side(place, triple, weight):
    shapes = [((ROWS, WIDTH), F32)] * 3
    return local(input_kernel, "input_side", shapes, flops=COST["small"])(place, triple, weight)


def merge_kernel(
    near_ref, behind_ref, line_ref, share_near, share_behind, up_ref, down_ref, near_out, behind_out
):
    near_out[:CUT] = (near_ref[:CUT] + up_ref[:CUT].astype(F32)).astype(BF16)
    near_out[CUT:ROWS] = near_ref[CUT:].astype(BF16)
    near_out[ROWS : ROWS + EXTRA] = line_ref[...]
    behind_out[:CUT] = behind_ref[:CUT].astype(BF16)
    behind_out[CUT:ROWS] = (
        behind_ref[CUT:] + down_ref[: ROWS - CUT].astype(F32)
    ).astype(BF16)
    lines = line_ref[...].astype(F32) + down_ref[ROWS - CUT : REST].astype(F32)
    behind_out[ROWS : ROWS + EXTRA] = split_line(
        jnp.sum(lines, axis=0, keepdims=True)
    ).astype(BF16)
    at = ROWS + EXTRA
    near_out[at : at + HALF] = (
        share_near[:HALF].astype(F32) + up_ref[CUT:].astype(F32)
    ).astype(BF16)
    near_out[at + HALF :] = share_near[HALF:]
    behind_out[at : at + HALF] = share_behind[:HALF]
    behind_out[at + HALF :] = (
        share_behind[HALF:].astype(F32) + down_ref[REST:].astype(F32)
    ).astype(BF16)


def merge(*args):
    shapes = [((2 * ROWS + EXTRA, WIDTH), BF16)] * 2
    return local(merge_kernel, "merge", shapes, place=False)(*args)


def finish_kernel(
    rest_ref, line_ref, share_ref, p1, p3, summed_ref, inv_ref, grad_ref, layer_ref, out_ref
):
    total = rest_ref[...] + p1[:ROWS].astype(F32) + p3[:ROWS].astype(F32)
    lines = line_ref[...].astype(F32)
    lines += p1[ROWS : ROWS + EXTRA].astype(F32) + p3[ROWS : ROWS + EXTRA].astype(F32)
    line = jnp.sum(lines[:, :ROWS], axis=0, keepdims=True) / (TP * WIDTH)
    centre = jnp.transpose(jnp.broadcast_to(line, (ROWS, ROWS)))[:, 0:1]
    inv = inv_ref[:, 0:1]
    summed = summed_ref[...].astype(F32)
    out_ref[...] = grad_ref[...].astype(F32) + inv * (total - summed * inv * centre)
    shares = (share_ref[...], p1[ROWS + EXTRA :], p3[ROWS + EXTRA :])
    layer_ref[...] = (summed + sum(share.astype(F32) for share in shares)).astype(BF16)


def finish(*args):
    shapes = [((ROWS, WIDTH), BF16), ((ROWS, WIDTH), F32)]
    return local(finish_kernel, "finish", shapes, place=False)(*args)


def ids_before(code_ids):
    route = [(i, i + 1) for i in range(lax.axis_size(SEQ) - 1)]
    return lax.ppermute(code_ids, SEQ, route)


def over_cores(block):
    return lax.ppermute(block, "core", [(0, 1), (1, 0)])


def body(code_ids, delays, embed_table, project_in, project_out, grad_output):
    place = [lax.axis_index(axis) for axis in ("y", "core", "tp")]
    place = jnp.stack(place + [lax.axis_index(SEQ) * ROWS]).astype(jnp.int32)
    place = jnp.concatenate([place, delays])
    weight_in = project_in.transpose(1, 0, 2)
    up_tp, down_tp = [lambda x, k=k: lax.ppermute(x, "tp", ring(k, TP)) for k in (1, -1)]
    up_y, down_y = [lambda x, k=k: lax.ppermute(x, "y", ring(k, 4)) for k in (1, -1)]
    together = lambda *values: lax.optimization_barrier(values)

    summed = embed(place, ids_before(code_ids), code_ids, embed_table)
    s1, s3 = up_tp(summed), down_tp(summed)
    summeds = [summed, s1, up_tp(s1), s3]
    grad, _ = together(grad_output, summed)
    g1, g3 = up_tp(grad), down_tp(grad)
    blocks, done, inv = project(place, summeds, weight_in)
    blocks, g1, g3 = together(blocks, g1, g3)
    mine = lax.all_to_all(blocks, HEADS_OVER, 0, 0, tiled=True)

    own, q_columns = prepare(mine)
    y1, y3, mate = up_y(own), down_y(own), over_cores(own)
    g2 = down_tp(g3)
    state = attend(0, place, q_columns, [(0, 0, own), (0, 1, mate)])
    y1, y3, g2, *state = together(y1, y3, g2, *state)
    other1, other3, y2 = over_cores(y1), over_cores(y3), up_y(y1)
    state = attend(1, place, q_columns, [(1, 0, y1), (3, 0, y3)], state)
    y2, *state = together(y2, *state)
    other2 = over_cores(y2)
    state = attend(2, place, q_columns, [(1, 1, other1), (3, 1, other3)], state)
    grads = [grad, g1, g2, g3]
    grad_heads = grad_side(place, grads, project_out)
    mixed, turned, stat = attend(
        3, place, q_columns, [(2, 0, y2), (2, 1, other2)], state, grad_heads
    )
    mixed = lax.all_to_all(mixed, HEADS_OVER, 0, 0, tiled=True)

    both, g_columns, delta = prepare_back(mixed, turned, q_columns, stat)
    held = (q_columns, g_columns, stat, delta)
    kept, sent, shares = output_side(place, mixed, grads, project_out)
    b1, b3, b_mate, got = up_y(both), down_y(both), over_cores(both), over_cores(sent)
    state = query_pass(
        place, held, [(0, 0, own), (0, 1, mate), (1, 0, y1), (1, 1, other1), (3, 0, y3)]
    )
    b1, b3, b_mate, got, state = together(b1, b3, b_mate, got, state)
    w0, w1, w2, w3 = core_sum(place, kept, got)
    w2, w3, b2 = up_y(w2), down_y(w3), up_y(b1)
    b_other1, b_other3 = over_cores(b1), over_cores(b3)
    query_grads, state = both_pass(
        place,
        held,
        [(2, 0, y2), (2, 1, other2), (3, 1, other3)],
        [(0, 0, both), (0, 1, b_mate), (1, 0, b1)],
        own,
        state,
    )
    w2, w3, b2, b_other1, b_other3, state = together(w2, w3, b2, b_other1, b_other3, state)
    w1, b_other2 = up_y(add(w1, w2)), over_cores(b2)
    state = pair_pass(
        place, own, [(3, 0, b3), (1, 1, b_other1), (3, 1, b_other3)], state
    )
    w1, b_other2, state = together(w1, b_other2, state)
    packed = last_pass(
        place, own, [(2, 0, b2), (2, 1, b_other2)], state, query_grads, w0, w1, w3
    )
    back = lax.all_to_all(packed, HEADS_OVER, 0, 0, tiled=True)

    triple, line, up, down = triple_side(place, back, done, shares[2], weight_in)
    up, down = up_tp(up), down_tp(down)
    near, behind, rest = input_side(place, triple, weight_in)
    near, behind = merge(near, behind, line, shares[1], shares[3], up, down)
    near, behind = up_tp(near), down_tp(behind)
    grad_project_out = weight_sum(back).transpose(1, 0)
    layer_output, grad_embed = finish(
        rest, line, shares[0], near, behind, summed, inv, grad_output
    )
    return layer_output, grad_embed, grad_project_out


def solution(mesh):
    fine = Mesh(mesh.devices.reshape(SPLIT), AXES)
    return jax.shard_map(
        body,
        mesh=fine,
        in_specs=(
            P(None, SEQ),
            P(),
            P(None, None, "tp"),
            P(None, None, "tp"),
            P("tp", None),
            P(SEQ, "tp"),
        ),
        out_specs=(P(SEQ, "tp"), P(SEQ, "tp"), P("tp", SEQ)),
        check_vma=False,
    )
```
